128 devices in a mesh: grp: 4 (over z), dev: 32 (over y, x, core).
Axes of the slice: x: 4, y: 4, z: 4, core: 2. Of those that a mesh axis runs over, the one named last changes fastest.
Arguments:
- inputs: bfloat16 [262144, 1536], P(('grp', 'dev')), may hold values from -6 to 6
- gate_in: bfloat16 [262144, 1536], P(('grp', 'dev')), may hold values from -6 to 6
- b_proj: bfloat16 [262144, 128], P(('grp', 'dev')), may hold values from -2 to 2
- c_proj: bfloat16 [262144, 128], P(('grp', 'dev')), may hold values from -2 to 2
- log_decay: float32 [24, 262144], P(None, ('grp', 'dev')), may hold values from -0.8 to 0
- d_skip: float32 [24], replicated, may hold values from 0.5 to 2
- norm_gain: float32 [1536], replicated, may hold values from 0.1 to 1.9
Outputs:
- result: bfloat16 [262144, 1536], P(('grp', 'dev'))
The draws below stay inside these ranges and needn't reach their ends.
All inputs are finite; a program needn't handle non-finite values.
Results may differ from the reference program's by a relative error of at most 0.0051.
Values sent between devices are 32-bit elements; how exact they have to be, the bound alone decides.
No kernel may reach another device: no remote copies, remote signals or barrier semaphores. Data moves between devices by JAX's collectives and lax.ppermute only.
A program may use at most 384 MiB of HBM per device.

```python
import jax
import jax.numpy as jnp
from jax import lax

ATTENTION_COUNT = 24
P_SIZE = 64
N = 128
Q = 256
TOK_DEV = 2048
SEQUENCE_SPAN = 262144


def draw_log_decay(key, part):
    key = jax.random.fold_in(key, 11)
    keys_all = jax.random.split(key, 6)
    share = 0.5
    slow_heads = jax.random.uniform(keys_all[0], (ATTENTION_COUNT,)) < share
    fast_rates = jnp.exp(jax.random.uniform(keys_all[1], (ATTENTION_COUNT,), jnp.float32, jnp.log(1.0 / 50.0), jnp.log(1.0 / 30.0)))
    per_channel_split = jnp.where(slow_heads, 0.7 / SEQUENCE_SPAN, fast_rates)
    approximate_guess = jax.random.uniform(keys_all[2], (ATTENTION_COUNT, SEQUENCE_SPAN), jnp.float32, 0.5, 1.5)
    multiplier_list = jnp.exp(jax.random.uniform(keys_all[3], (ATTENTION_COUNT, SEQUENCE_SPAN // TOK_DEV), jnp.float32, jnp.log(0.5), jnp.log(2.0)))
    multiplier_list = jnp.repeat(multiplier_list, TOK_DEV, axis=1)
    location_indices = jax.random.randint(keys_all[4], (2,), 0, SEQUENCE_SPAN)
    layer_tiers = jnp.log(jax.random.uniform(keys_all[5], (2, ATTENTION_COUNT), jnp.float32, 0.5, 0.8))
    segment_sets = jnp.zeros((ATTENTION_COUNT, SEQUENCE_SPAN), jnp.float32).at[:, location_indices].add(layer_tiers.T)
    return (-per_channel_split[:, None] * approximate_guess * multiplier_list + segment_sets).astype(jnp.float32)


def levels(rng, shape, pieces, least, top_value):
    factor_of = 1.0
    for axis_at, parts in pieces:
        heights = jax.random.uniform(jax.random.fold_in(jax.random.fold_in(rng, 6), axis_at), (parts,), jnp.float32, least / len(pieces), top_value / len(pieces))
        factor_of = factor_of * jnp.repeat(jnp.exp(heights), shape[axis_at] // parts).reshape((-1,) + (1,) * (len(shape) - 1 - axis_at))
    return factor_of


def gaussian(own_key, shape, deviation, reach, cuts=(), kind=jnp.bfloat16):
    result = jax.random.normal(own_key, shape, jnp.float32) * deviation
    if len(cuts) > 0:
        result = levels(own_key, shape, cuts, -0.22, 0.18) * result
    return jnp.clip(result, min=-reach, max=reach).astype(kind)


def setup_inputs(seed: int = 0) -> dict:
    splits = jax.random.split(jax.random.key(seed), 8)
    inputs = gaussian(splits[0], (SEQUENCE_SPAN, ATTENTION_COUNT * P_SIZE), 1.0, 6.0, ((0, 128),))
    gate_in = gaussian(splits[1], (SEQUENCE_SPAN, ATTENTION_COUNT * P_SIZE), 1.0, 6.0, ((0, 128),))
    b_proj = gaussian(splits[2], (SEQUENCE_SPAN, N), 0.3, 2.0, ((0, 128),))
    c_proj = gaussian(splits[3], (SEQUENCE_SPAN, N), 0.3, 2.0, ((0, 128),))
    log_decay = draw_log_decay(jax.random.fold_in(splits[7], 71), 0)
    d_skip = jnp.clip(jax.random.uniform(splits[5], (ATTENTION_COUNT,), jnp.float32, 0.5, 2.0), 0.5, 2.0)
    norm_gain = jnp.clip(1.0 + 0.18 * jax.random.normal(splits[6], (ATTENTION_COUNT * P_SIZE,), jnp.float32), 0.1, 1.9)
    return {"inputs": inputs, "gate_in": gate_in, "b_proj": b_proj, "c_proj": c_proj, "log_decay": log_decay, "d_skip": d_skip, "norm_gain": norm_gain}


def reference(inputs, gate_in, b_proj, c_proj, log_decay, d_skip, norm_gain):
    row_count = inputs.shape[0]
    blocks = row_count // Q
    values = inputs.reshape(blocks, Q, ATTENTION_COUNT, P_SIZE)
    gates = gate_in.reshape(blocks, Q, ATTENTION_COUNT, P_SIZE)
    b_blocks = b_proj.reshape(blocks, Q, N)
    c_blocks = c_proj.reshape(blocks, Q, N)
    decays = log_decay.reshape(ATTENTION_COUNT, blocks, Q).transpose(1, 0, 2)
    causal = jnp.tril(jnp.ones((Q, Q), dtype=bool))
    gains = norm_gain.reshape(ATTENTION_COUNT, P_SIZE)

    def advance(running, element):
        piece, gate_piece, b_rows, c_rows, decay_rows = element
        cumul = jnp.cumsum(decay_rows, axis=1)
        scores = jnp.dot(c_rows, b_rows.T, preferred_element_type=jnp.float32)
        spread = jnp.where(causal[None], cumul[:, :, None] - cumul[:, None, :], -jnp.inf)
        weight = (scores[None] * jnp.exp(spread)).astype(jnp.bfloat16)
        within = jnp.einsum('hts,shp->thp', weight.astype(jnp.float32), piece.astype(jnp.float32))
        rounded = running.astype(jnp.bfloat16)
        carried = jnp.einsum('qn,hnp->qhp', c_rows.astype(jnp.float32), rounded.astype(jnp.float32))
        carried = carried * jnp.exp(cumul).T[:, :, None]
        summed = within + carried + d_skip[None, :, None] * piece.astype(jnp.float32)
        gated_out = summed * jax.nn.silu(gate_piece.astype(jnp.float32))
        inverse = lax.rsqrt(lax.optimization_barrier(jnp.mean(gated_out * gated_out, axis=-1, keepdims=True)) + 1e-05)
        output = (gated_out * inverse * gains[None]).astype(jnp.bfloat16)
        fading = jnp.exp(cumul[:, -1:] - cumul)
        scaled_b = (fading[:, :, None] * b_rows.astype(jnp.float32)[None]).astype(jnp.bfloat16)
        summary = jnp.einsum('hqn,qhp->hnp', scaled_b.astype(jnp.float32), piece.astype(jnp.float32))
        updated = jnp.exp(cumul[:, -1])[:, None, None] * running + summary
        return (updated, output)
    start = jnp.zeros((ATTENTION_COUNT, N, P_SIZE), jnp.float32)
    final_state, outputs = lax.scan(advance, start, (values, gates, b_blocks, c_blocks, decays))
    return outputs.reshape(row_count, ATTENTION_COUNT * P_SIZE)
```

```python
import jax
import jax.numpy as jnp
from jax import lax
from jax.experimental import pallas as pl
from jax.experimental.pallas import tpu as pltpu
from jax.sharding import PartitionSpec as P

HEADS = 24
HEAD = 64
STATE = 128
WIDTH = HEADS * HEAD
HALF = WIDTH // 2
SUB = 128
STEP = 256
GROUP = 256
ROWS = STATE + 8
SHIFT = 74
SHIFT_LOG = 51.29289136
GRID = 8
QUARTER = STATE // 4
F32 = jnp.float32
BF16 = jnp.bfloat16


def dot(a, b, dims=((1,), (0,))):
    return lax.dot_general(a, b, (dims, ((), ())), preferred_element_type=F32)


def iota(shape, dim):
    return lax.broadcasted_iota(jnp.int32, shape, dim)


def three(v):
    high = v.astype(BF16)
    rest = v - high.astype(F32)
    middle = rest.astype(BF16)
    low = (rest - middle.astype(F32)).astype(BF16)
    return high, middle, low


def spread_parts(v):
    high, middle, low = three(v)
    lane = iota(v.shape, 1)
    picked = jnp.where(
        lane < HEADS, high.astype(F32), jnp.where(lane < 2 * HEADS, middle.astype(F32), low.astype(F32))
    )
    return picked.astype(BF16)


def decay_sums(matrix, decay):
    high, middle, low = three(decay)
    nt = ((1,), (1,))
    return dot(matrix, high, nt) + (dot(matrix, middle, nt) + dot(matrix, low, nt))


def spread_matrix():
    k = iota((3 * HEADS, WIDTH), 0)
    head = iota((3 * HEADS, WIDTH), 1) // HEAD
    hit = (k == head) | (k == head + HEADS) | (k == head + 2 * HEADS)
    return jnp.where(hit, 1.0, 0.0).astype(BF16)


def end_state_kernel(core_ref, x_ref, b_ref, decay_ref, spread_ref, keep_ref, send_ref, acc):
    step = pl.program_id(0)

    @pl.when(step == 0)
    def _():
        acc[:STATE] = jnp.zeros((STATE, WIDTH), F32)
        acc[STATE:] = jnp.ones((8, WIDTH), F32)

    decay = decay_ref[...]
    decay = jnp.concatenate([decay] * 3, axis=0)
    row, col = iota((STEP + 16, STEP), 0), iota((STEP + 16, STEP), 1)
    later = jnp.where((col > row) | (row >= STEP), 1.0, 0.0).astype(BF16)
    factors = spread_parts(jnp.exp(decay_sums(later, decay)))
    b = b_ref[...]
    for g in range(WIDTH // GROUP):
        lanes = slice(g * GROUP, (g + 1) * GROUP)
        wide = dot(factors, spread_ref[:, lanes])
        scaled = (x_ref[:, lanes].astype(F32) * wide[:STEP]).astype(BF16)
        total = wide[STEP : STEP + 1]
        acc[:STATE, lanes] = acc[:STATE, lanes] * total + dot(b, scaled, ((0,), (0,)))
        acc[STATE:, lanes] = acc[STATE:, lanes] * total

    @pl.when(step == pl.num_programs(0) - 1)
    def _():
        mine = pl.multiple_of(core_ref[0] * HALF, HALF)
        other = pl.multiple_of((1 - core_ref[0]) * HALF, HALF)
        keep_ref[...] = acc[:, pl.ds(mine, HALF)]
        send_ref[...] = acc[:, pl.ds(other, HALF)]


def end_state(core, x, b, decay, spread):
    tokens = x.shape[0]
    half = jax.ShapeDtypeStruct((ROWS, HALF), F32)
    return pl.pallas_call(
        end_state_kernel,
        grid_spec=pltpu.PrefetchScalarGridSpec(
            num_scalar_prefetch=1,
            grid=(tokens // STEP,),
            in_specs=[
                pl.BlockSpec((STEP, WIDTH), lambda i, c: (i, 0)),
                pl.BlockSpec((STEP, STATE), lambda i, c: (i, 0)),
                pl.BlockSpec((HEADS, STEP), lambda i, c: (0, i)),
                pl.BlockSpec((3 * HEADS, WIDTH), lambda i, c: (0, 0)),
            ],
            out_specs=[
                pl.BlockSpec((ROWS, HALF), lambda i, c: (0, 0)),
                pl.BlockSpec((ROWS, HALF), lambda i, c: (0, 0)),
            ],
            scratch_shapes=[pltpu.VMEM((ROWS, WIDTH), F32)],
        ),
        out_shape=[half, half],
        name="end_state",
        compiler_params=pltpu.CompilerParams(vmem_limit_bytes=40 * 1024 * 1024),
    )(core, x, b, decay, spread)


def small_call(kernel, name, place, args, outs):
    vmem = pl.BlockSpec(memory_space=pltpu.VMEM)
    return pl.pallas_call(
        kernel,
        in_specs=[pl.BlockSpec(memory_space=pltpu.SMEM)] + [vmem] * len(args),
        out_specs=[vmem] * len(outs),
        out_shape=[jax.ShapeDtypeStruct(s, F32) for s in outs],
        name=name,
    )(place, *args)


Z, Y, X, CORE = 0, 1, 2, 3


def pair_kernel(place, keep, recv, own, *sends):
    flip = place[CORE] == 1
    kept, got = keep[STATE : STATE + 8], recv[STATE : STATE + 8]
    late = jnp.where(flip, kept, got)[:1]
    decay = kept * got
    for shift, out in enumerate((own,) + sends):
        chunk = (place[X] + shift) % 4
        rows = pl.ds(pl.multiple_of(chunk * QUARTER, QUARTER), QUARTER)
        a, b = keep[rows], recv[rows]
        out[:QUARTER] = late * jnp.where(flip, b, a) + jnp.where(flip, a, b)
        out[QUARTER:] = decay


def ordered(place, axis, refs, j):
    shift = (place[axis] - j + 4) % 4
    value = refs[0][...]
    for s in (1, 2, 3):
        value = jnp.where(shift == s, refs[s][...], value)
    return value


def line_kernel(place, u0, u1, u2, u3, total):
    state = jnp.zeros((QUARTER, HALF), F32)
    decay = jnp.ones((8, HALF), F32)
    for j in range(4):
        u = ordered(place, X, (u0, u1, u2, u3), j)
        state = u[QUARTER : QUARTER + 1] * state + u[:QUARTER]
        decay = decay * u[QUARTER:]
    total[:QUARTER] = state
    total[QUARTER:] = decay


def plane_kernel(place, v0, v1, v2, v3, total, before):
    state = jnp.zeros((QUARTER, HALF), F32)
    decay = jnp.ones((8, HALF), F32)
    for j in range(4):

        @pl.when(place[Y] == j)
        def _(state=state, decay=decay):
            before[:QUARTER] = state
            before[QUARTER:] = decay

        v = ordered(place, Y, (v0, v1, v2, v3), j)
        state = v[QUARTER : QUARTER + 1] * state + v[:QUARTER]
        decay = decay * v[QUARTER:]
    total[:QUARTER] = state
    total[QUARTER:] = decay


def enter_kernel(place, w0, w1, w2, w3, before, u0, u1, u2, u3, own, *sends):
    state = jnp.zeros((QUARTER, HALF), F32)
    for j in range(3):
        w = ordered(place, Z, (w0, w1, w2, w3), j)
        updated = w[QUARTER : QUARTER + 1] * state + w[:QUARTER]
        state = jnp.where(j < place[Z], updated, state)
    state = before[QUARTER : QUARTER + 1] * state + before[:QUARTER]
    for j in range(4):
        for shift, out in enumerate((own,) + sends):

            @pl.when((place[X] + shift) % 4 == j)
            def _(state=state, out=out):
                out[...] = state

        if j < 3:
            u = ordered(place, X, (u0, u1, u2, u3), j)
            state = u[QUARTER : QUARTER + 1] * state + u[:QUARTER]


def chip_kernel(place, e0, e1, e2, e3, keep, recv, own, send):
    flip = place[CORE] == 1
    first = jnp.where(flip, recv[STATE : STATE + 1], keep[STATE : STATE + 1])
    for shift, e in enumerate((e0, e1, e2, e3)):
        chunk = (place[X] - shift + 4) % 4
        rows = pl.ds(pl.multiple_of(chunk * QUARTER, QUARTER), QUARTER)
        at_first = e[...]
        at_second = first * at_first + jnp.where(flip, recv[rows], keep[rows])
        own[rows] = jnp.where(flip, at_second, at_first)
        send[rows] = jnp.where(flip, at_first, at_second)


def output_kernel(
    core_ref, x_ref, gate_ref, b_ref, c_ref, decay_ref, spread_ref, skip_ref, gain_ref, own_ref, other_ref,
    out_ref, state,
):
    @pl.when(pl.program_id(0) == 0)
    def _():
        mine = pl.multiple_of(core_ref[0] * HALF, HALF)
        other = pl.multiple_of((1 - core_ref[0]) * HALF, HALF)
        state[:, pl.ds(mine, HALF)] = own_ref[...]
        state[:, pl.ds(other, HALF)] = other_ref[...]

    row, col = iota((SUB, SUB), 0), iota((SUB, SUB), 1)
    causal = col <= row
    upto = jnp.where(causal, 1.0, 0.0).astype(BF16)
    same = iota((GROUP, GROUP), 0) // HEAD == iota((GROUP, GROUP), 1) // HEAD
    mean = jnp.where(same, 1.0 / HEAD, 0.0).astype(BF16)
    down = 2.0**-SHIFT
    for s in range(STEP // SUB):
        rows = slice(s * SUB, (s + 1) * SUB)
        decay = decay_ref[:, rows]
        cumul = decay_sums(upto, jnp.concatenate([decay] * 3, axis=0))
        at_end = cumul[SUB - 1 : SUB] + SHIFT_LOG
        exponents = jnp.concatenate([at_end - cumul, cumul - at_end, jnp.broadcast_to(at_end, (16, 3 * HEADS))], axis=0)
        factors = spread_parts(jnp.exp(exponents))
        b, c = b_ref[rows], c_ref[rows]
        scores = jnp.where(causal, dot(c, b, ((1,), (1,))), 0.0).astype(BF16)
        b_t = jnp.transpose(b.astype(F32)).astype(BF16)
        upper = jnp.concatenate([scores, c], axis=1)
        lower = jnp.concatenate([b_t, jnp.zeros((STATE, STATE), BF16)], axis=1)
        left = jnp.concatenate([upper, lower], axis=0)
        for g in range(WIDTH // GROUP):
            lanes = slice(g * GROUP, (g + 1) * GROUP)
            wide = dot(factors, spread_ref[:, lanes])
            x = x_ref[rows, lanes].astype(F32)
            scaled = (x * wide[:SUB]).astype(BF16)
            carried = state[:, lanes] * wide[2 * SUB : 2 * SUB + 1]
            both = dot(left, jnp.concatenate([scaled, carried.astype(BF16)], axis=0))
            state[:, lanes] = (carried + both[SUB:]) * down
            summed = both[:SUB] * wide[SUB : 2 * SUB] + skip_ref[:, lanes] * x
            h = 0.5 * gate_ref[rows, lanes].astype(F32)
            gated = summed * (h + h * jnp.tanh(h))
            square = dot((gated * gated).astype(BF16), mean)
            out = gated * lax.rsqrt(square + 1e-5) * gain_ref[:, lanes]
            out_ref[rows, lanes] = out.astype(BF16)


def output(core, x, gate, b, c, decay, spread, skip, gain, own, other):
    tokens = x.shape[0]
    wide = pl.BlockSpec((STEP, WIDTH), lambda i, c: (i, 0))
    narrow = pl.BlockSpec((STEP, STATE), lambda i, c: (i, 0))
    line = pl.BlockSpec((1, WIDTH), lambda i, c: (0, 0))
    half = pl.BlockSpec((STATE, HALF), lambda i, c: (0, 0))
    return pl.pallas_call(
        output_kernel,
        grid_spec=pltpu.PrefetchScalarGridSpec(
            num_scalar_prefetch=1,
            grid=(tokens // STEP,),
            in_specs=[
                wide, wide, narrow, narrow,
                pl.BlockSpec((HEADS, STEP), lambda i, c: (0, i)),
                pl.BlockSpec((3 * HEADS, WIDTH), lambda i, c: (0, 0)),
                line, line, half, half,
            ],
            out_specs=wide,
            scratch_shapes=[pltpu.VMEM((STATE, WIDTH), F32)],
        ),
        out_shape=jax.ShapeDtypeStruct((tokens, WIDTH), BF16),
        name="output",
        compiler_params=pltpu.CompilerParams(vmem_limit_bytes=40 * 1024 * 1024),
    )(core, x, gate, b, c, decay, spread, skip, gain, own, other)


def device_of(z, y, x, core):
    return ((z * 4 + y) * 4 + x) * 2 + core


def moved(value, axis, shift):
    sizes = (4, 4, 4, 2)
    pairs = []
    for z in range(4):
        for y in range(4):
            for x in range(4):
                for core in range(2):
                    to = [z, y, x, core]
                    to[axis] = (to[axis] + shift) % sizes[axis]
                    pairs.append((device_of(z, y, x, core), device_of(*to)))
    return lax.ppermute(value, ("grp", "dev"), pairs)


def on_device(x, gate, b, c, decay, d_skip, norm_gain):
    z, r = lax.axis_index("grp"), lax.axis_index("dev")
    place = jnp.stack([z, r // 8, (r // 2) % 4, r % 2]).astype(jnp.int32)
    core = place[CORE:]
    spread = spread_matrix()
    piece, chunk = (QUARTER + 8, HALF), (QUARTER, HALF)

    keep, send = end_state(core, x, b, decay, spread)
    recv = moved(send, CORE, 1)
    u0, *sends = small_call(pair_kernel, "pair", place, (keep, recv), [piece] * 4)
    lines = [u0] + [moved(v, X, s + 1) for s, v in enumerate(sends)]
    (v0,) = small_call(line_kernel, "line", place, lines, [piece])
    columns = [v0] + [moved(v0, Y, s) for s in (1, 2, 3)]
    w0, before = small_call(plane_kernel, "plane", place, columns, [piece] * 2)
    planes = [w0] + [moved(w0, Z, s) for s in (1, 2, 3)]
    e0, *sends = small_call(enter_kernel, "enter", place, planes + [before] + lines, [chunk] * 4)
    entering = [e0] + [moved(v, X, s + 1) for s, v in enumerate(sends)]
    own, send = small_call(chip_kernel, "chip", place, entering + [keep, recv], [(STATE, HALF)] * 2)
    other = moved(send, CORE, 1)
    skip = jnp.repeat(d_skip, HEAD)[None]
    return output(core, x, gate, b, c, decay, spread, skip, norm_gain[None], own, other)


def solution(mesh):
    return jax.shard_map(
        on_device,
        mesh=mesh,
        in_specs=(
            P(("grp", "dev"), None),
            P(("grp", "dev"), None),
            P(("grp", "dev"), None),
            P(("grp", "dev"), None),
            P(None, ("grp", "dev")),
            P(),
            P(),
        ),
        out_specs=P(("grp", "dev"), None),
        check_vma=False,
    )
```

```python
import functools

import jax
import jax.numpy as jnp
from jax import lax
from jax.experimental import pallas as pl
from jax.experimental.pallas import tpu as pltpu
from jax.sharding import PartitionSpec as P

HEADS = 24
HEAD = 64
STATE = 128
WIDTH = HEADS * HEAD
HALF = WIDTH // 2
SUB = 128
STEP = 256
GROUP = 256
ROWS = STATE + 8
SHIFT = 74
SHIFT_LOG = 51.29289136
OUT_STEP = 256
QUARTER = STATE // 4
FIRST_LIMIT = 60 * 1024 * 1024
LIMIT = 18 * 1024 * 1024
SMALL_LIMIT = 6 * 1024 * 1024
F32 = jnp.float32
BF16 = jnp.bfloat16


def dot(a, b, dims=((1,), (0,))):
    return lax.dot_general(a, b, (dims, ((), ())), preferred_element_type=F32)


def iota(shape, dim):
    return lax.broadcasted_iota(jnp.int32, shape, dim)


def three(v):
    high = v.astype(BF16)
    rest = v - high.astype(F32)
    middle = rest.astype(BF16)
    low = (rest - middle.astype(F32)).astype(BF16)
    return high, middle, low


def spread_parts(v):
    high, middle, low = three(v)
    lane = iota(v.shape, 1)
    picked = jnp.where(
        lane < HEADS, high.astype(F32), jnp.where(lane < 2 * HEADS, middle.astype(F32), low.astype(F32))
    )
    return picked.astype(BF16)


def decay_sums(matrix, decay):
    high, middle, low = three(decay)
    nt = ((1,), (1,))
    return dot(matrix, high, nt) + (dot(matrix, middle, nt) + dot(matrix, low, nt))


def spread_matrix(start, width):
    k, lane = iota((3 * HEADS, width), 0), start + iota((3 * HEADS, width), 1)
    return jnp.where(k % HEADS == lane // HEAD, 1.0, 0.0).astype(BF16)


def end_state_kernel(place, x_hbm, b_hbm, decay_hbm, keep_ref, send_ref, x, b, decay, scaled, factors, spread, sems):
    steps = x.shape[0] // STEP
    fetch_decay = pltpu.make_async_copy(decay_hbm, decay, sems.at[steps])
    fetch_decay.start()
    copies = []
    for i in range(steps):
        rows = pl.ds(i * STEP, STEP)
        copies.append(pltpu.make_async_copy(x_hbm.at[rows], x.at[rows], sems.at[i]))
        copies[-1].start()
    fetch_b = pltpu.make_async_copy(b_hbm, b, sems.at[steps + 1])
    fetch_b.start()
    spread[...] = spread_matrix(0, WIDTH)
    row, col = iota((STEP + 16, STEP), 0), iota((STEP + 16, STEP), 1)
    later = jnp.where((col > row) | (row >= STEP), 1.0, 0.0).astype(BF16)
    fetch_decay.wait()
    sums = []
    for i in range(steps):
        part = decay[:, i * STEP : (i + 1) * STEP]
        sums.append(decay_sums(later, jnp.concatenate([part] * 3, axis=0)))
    after = jnp.zeros((1, 3 * HEADS), F32)
    for i in reversed(range(steps)):
        factors[i * STEP : (i + 1) * STEP] = spread_parts(jnp.exp(sums[i][:STEP] + after))
        after = after + sums[i][STEP : STEP + 1]
    whole = spread_parts(jnp.exp(jnp.broadcast_to(after, (16, 3 * HEADS))))
    for i in range(steps):
        copies[i].wait()
        rows = slice(i * STEP, (i + 1) * STEP)
        scaled[rows] = (x[rows].astype(F32) * dot(factors[rows], spread[...])).astype(BF16)
    fetch_b.wait()
    mine = pl.multiple_of(place[CORE] * HALF, HALF)
    other = pl.multiple_of((1 - place[CORE]) * HALF, HALF)
    for start, out in ((other, send_ref), (mine, keep_ref)):
        lanes = pl.ds(start, HALF)
        out[:STATE] = dot(b[...], scaled[:, lanes], ((0,), (0,)))
        out[STATE:] = dot(whole, spread[:, lanes])[:8]


def end_state(place, x, b, decay):
    tokens = x.shape[0]
    half = jax.ShapeDtypeStruct((ROWS, HALF), F32)
    vmem = pl.BlockSpec(memory_space=pltpu.VMEM)
    return pl.pallas_call(
        end_state_kernel,
        in_specs=[pl.BlockSpec(memory_space=pltpu.SMEM)] + [pl.BlockSpec(memory_space=pl.ANY)] * 3,
        out_specs=[vmem, vmem],
        out_shape=[half, half],
        scratch_shapes=[
            pltpu.VMEM(x.shape, BF16),
            pltpu.VMEM(b.shape, BF16),
            pltpu.VMEM(decay.shape, F32),
            pltpu.VMEM((tokens, WIDTH), BF16),
            pltpu.VMEM((tokens, 3 * HEADS), BF16),
            pltpu.VMEM((3 * HEADS, WIDTH), BF16),
            pltpu.SemaphoreType.DMA((tokens // STEP + 2,)),
        ],
        name="end_state",
        compiler_params=pltpu.CompilerParams(vmem_limit_bytes=FIRST_LIMIT),
    )(place, x, b, decay)


def small_call(kernel, name, place, args, outs):
    vmem = pl.BlockSpec(memory_space=pltpu.VMEM)
    return pl.pallas_call(
        kernel,
        in_specs=[pl.BlockSpec(memory_space=pltpu.SMEM)] + [vmem] * len(args),
        out_specs=[vmem] * len(outs),
        out_shape=[jax.ShapeDtypeStruct(s, F32) for s in outs],
        name=name,
        compiler_params=pltpu.CompilerParams(vmem_limit_bytes=SMALL_LIMIT),
    )(place, *args)


Z, Y, X, CORE = 0, 1, 2, 3


def pair_kernel(place, keep, recv, own, *sends):
    flip = place[CORE] == 1
    kept, got = keep[STATE : STATE + 8], recv[STATE : STATE + 8]
    late = jnp.where(flip, kept, got)[:1]
    decay = kept * got
    for shift, out in enumerate((own,) + sends):
        chunk = (place[X] + shift) % 4
        rows = pl.ds(pl.multiple_of(chunk * QUARTER, QUARTER), QUARTER)
        a, b = keep[rows], recv[rows]
        out[:QUARTER] = late * jnp.where(flip, b, a) + jnp.where(flip, a, b)
        out[QUARTER:] = decay


def ordered(place, axis, refs, j):
    shift = (place[axis] - j + 4) % 4
    value = refs[0][...]
    for s in (1, 2, 3):
        value = jnp.where(shift == s, refs[s][...], value)
    return value


def line_kernel(place, u0, u1, u2, u3, total):
    state = jnp.zeros((QUARTER, HALF), F32)
    decay = jnp.ones((8, HALF), F32)
    for j in range(4):
        u = ordered(place, X, (u0, u1, u2, u3), j)
        state = u[QUARTER : QUARTER + 1] * state + u[:QUARTER]
        decay = decay * u[QUARTER:]
    total[:QUARTER] = state
    total[QUARTER:] = decay


def plane_kernel(place, v0, v1, v2, v3, total, before):
    state = jnp.zeros((QUARTER, HALF), F32)
    decay = jnp.ones((8, HALF), F32)
    for j in range(4):

        @pl.when(place[Y] == j)
        def _(state=state, decay=decay):
            before[:QUARTER] = state
            before[QUARTER:] = decay

        v = ordered(place, Y, (v0, v1, v2, v3), j)
        state = v[QUARTER : QUARTER + 1] * state + v[:QUARTER]
        decay = decay * v[QUARTER:]
    total[:QUARTER] = state
    total[QUARTER:] = decay


def enter_kernel(place, w0, w1, w2, w3, before, u0, u1, u2, u3, own, *sends):
    state = jnp.zeros((QUARTER, HALF), F32)
    for j in range(3):
        w = ordered(place, Z, (w0, w1, w2, w3), j)
        updated = w[QUARTER : QUARTER + 1] * state + w[:QUARTER]
        state = jnp.where(j < place[Z], updated, state)
    state = before[QUARTER : QUARTER + 1] * state + before[:QUARTER]
    for j in range(4):
        for shift, out in enumerate((own,) + sends):

            @pl.when((place[X] + shift) % 4 == j)
            def _(state=state, out=out):
                out[...] = state

        if j < 3:
            u = ordered(place, X, (u0, u1, u2, u3), j)
            state = u[QUARTER : QUARTER + 1] * state + u[:QUARTER]


def chip_kernel(place, e0, e1, e2, e3, keep, recv, own, send):
    flip = place[CORE] == 1
    first = jnp.where(flip, recv[STATE : STATE + 1], keep[STATE : STATE + 1])
    for shift, e in enumerate((e0, e1, e2, e3)):
        chunk = (place[X] - shift + 4) % 4
        rows = pl.ds(pl.multiple_of(chunk * QUARTER, QUARTER), QUARTER)
        at_first = e[...]
        at_second = first * at_first + jnp.where(flip, recv[rows], keep[rows])
        own[rows] = jnp.where(flip, at_second, at_first)
        send[rows] = jnp.where(flip, at_first, at_second)


FACTORS = 3 * SUB + 16


def prepare_kernel(b_ref, c_ref, decay_ref, left_ref, b_t_ref, factors_ref):
    tokens = b_ref.shape[0]
    row, col = iota((SUB, SUB), 0), iota((SUB, SUB), 1)
    causal = col <= row
    upto = jnp.where(causal, 1.0, 0.0).astype(BF16)
    before = jnp.zeros((1, 3 * HEADS), F32)
    for s in range(tokens // SUB):
        rows = slice(s * SUB, (s + 1) * SUB)
        decay = decay_ref[:, rows]
        cumul = decay_sums(upto, jnp.concatenate([decay] * 3, axis=0))
        end = cumul[SUB - 1 : SUB]
        shifted = end + SHIFT_LOG
        exponents = [shifted - cumul, jnp.broadcast_to(shifted, (16, 3 * HEADS)), cumul - shifted, cumul + before]
        factors_ref[s] = spread_parts(jnp.exp(jnp.concatenate(exponents, axis=0)))
        before = before + end
        b, c = b_ref[rows], c_ref[rows]
        scores = jnp.where(causal, dot(c, b, ((1,), (1,))), 0.0)
        left_ref[rows, :SUB] = scores.astype(BF16)
        left_ref[rows, SUB:] = c
        b_t_ref[rows] = jnp.transpose(b.astype(F32)).astype(BF16)


def prepare(b, c, decay):
    tokens = b.shape[0]
    vmem = pl.BlockSpec(memory_space=pltpu.VMEM)
    return pl.pallas_call(
        prepare_kernel,
        in_specs=[vmem] * 3,
        out_specs=[vmem] * 3,
        out_shape=[
            jax.ShapeDtypeStruct((tokens, SUB + STATE), BF16),
            jax.ShapeDtypeStruct((tokens, SUB), BF16),
            jax.ShapeDtypeStruct((tokens // SUB, FACTORS, 3 * HEADS), BF16),
        ],
        name="prepare",
        compiler_params=pltpu.CompilerParams(vmem_limit_bytes=LIMIT),
    )(b, c, decay)


def local_kernel(group, skip_ref, x_ref, gate_ref, left_ref, b_t_ref, factors_ref, sum_ref, weight_ref, scaled, carried):
    tokens = x_ref.shape[0]
    lanes = slice(group * GROUP, (group + 1) * GROUP)
    spread = spread_matrix(group * GROUP, GROUP)
    lane = iota((1, GROUP), 1)
    skip = jnp.zeros((1, GROUP), F32)
    for h in range(GROUP // HEAD):
        skip = jnp.where(lane // HEAD == h, skip_ref[group * (GROUP // HEAD) + h], skip)
    state = jnp.zeros((STATE, GROUP), F32)
    down = 2.0**-SHIFT
    for s in range(tokens // SUB):
        rows = slice(s * SUB, (s + 1) * SUB)
        wide = dot(factors_ref[s, : SUB + 16], spread)
        scaled[rows] = (x_ref[rows, lanes].astype(F32) * wide[:SUB]).astype(BF16)
        decayed = state * wide[SUB : SUB + 1]
        carried[rows] = decayed.astype(BF16)
        state = (decayed + dot(b_t_ref[rows], scaled[rows])) * down
    for s in range(tokens // SUB):
        rows = slice(s * SUB, (s + 1) * SUB)
        wide = dot(factors_ref[s, SUB + 16 :], spread)
        own = dot(left_ref[rows], jnp.concatenate([scaled[rows], carried[rows]], axis=0))
        summed = own * wide[:SUB] + skip * x_ref[rows, lanes].astype(F32)
        h = 0.5 * gate_ref[rows, lanes].astype(F32)
        silu = h + h * jnp.tanh(h)
        sum_ref[rows] = (summed * silu).astype(sum_ref.dtype)
        weight_ref[rows] = (wide[SUB:] * silu).astype(weight_ref.dtype)


def local(group, skip, x, gate, left, b_t, factors):
    tokens = x.shape[0]
    vmem = pl.BlockSpec(memory_space=pltpu.VMEM)
    return pl.pallas_call(
        functools.partial(local_kernel, group),
        in_specs=[pl.BlockSpec(memory_space=pltpu.SMEM)] + [vmem] * 5,
        out_specs=[vmem] * 2,
        out_shape=[jax.ShapeDtypeStruct((tokens, GROUP), F32), jax.ShapeDtypeStruct((tokens, GROUP), BF16)],
        scratch_shapes=[pltpu.VMEM((tokens, GROUP), BF16)] * 2,
        name="local",
        compiler_params=pltpu.CompilerParams(vmem_limit_bytes=LIMIT),
    )(skip, x, gate, left, b_t, factors)


def output_kernel(place, c_ref, gain_ref, own_ref, other_ref, *refs):
    groups = WIDTH // GROUP
    sums, weights = refs[:groups], refs[groups : 2 * groups]
    out_hbm, state, out, sems = refs[2 * groups :]
    mine = pl.multiple_of(place[CORE] * HALF, HALF)
    other = pl.multiple_of((1 - place[CORE]) * HALF, HALF)
    state[:, pl.ds(mine, HALF)] = own_ref[...].astype(BF16)
    state[:, pl.ds(other, HALF)] = other_ref[...].astype(BF16)
    same = iota((GROUP, GROUP), 0) // HEAD == iota((GROUP, GROUP), 1) // HEAD
    mean = jnp.where(same, 1.0 / HEAD, 0.0).astype(BF16)
    copies = []
    for i in range(out.shape[0] // OUT_STEP):
        rows = slice(i * OUT_STEP, (i + 1) * OUT_STEP)
        for g in range(groups):
            lanes = slice(g * GROUP, (g + 1) * GROUP)
            entering = dot(c_ref[rows], state[:, lanes])
            gated = sums[g][rows].astype(F32) + weights[g][rows].astype(F32) * entering
            square = dot((gated * gated).astype(BF16), mean)
            out[rows, lanes] = (gated * lax.rsqrt(square + 1e-5) * gain_ref[:, lanes]).astype(BF16)
        where = pl.ds(i * OUT_STEP, OUT_STEP)
        copies.append(pltpu.make_async_copy(out.at[where], out_hbm.at[where], sems.at[i]))
        copies[-1].start()
    for copy in copies:
        copy.wait()


def output(place, c, gain, own, other, sums, weights):
    tokens = c.shape[0]
    vmem = pl.BlockSpec(memory_space=pltpu.VMEM)
    return pl.pallas_call(
        output_kernel,
        in_specs=[pl.BlockSpec(memory_space=pltpu.SMEM)] + [vmem] * (4 + len(sums) + len(weights)),
        out_specs=pl.BlockSpec(memory_space=pl.ANY),
        out_shape=jax.ShapeDtypeStruct((tokens, WIDTH), BF16),
        scratch_shapes=[
            pltpu.VMEM((STATE, WIDTH), BF16),
            pltpu.VMEM((tokens, WIDTH), BF16),
            pltpu.SemaphoreType.DMA((tokens // OUT_STEP,)),
        ],
        name="output",
        compiler_params=pltpu.CompilerParams(vmem_limit_bytes=LIMIT),
    )(place, c, gain, own, other, *sums, *weights)


def device_of(z, y, x, core):
    return ((z * 4 + y) * 4 + x) * 2 + core


def moved(value, axis, shift):
    sizes = (4, 4, 4, 2)
    pairs = []
    for z in range(4):
        for y in range(4):
            for x in range(4):
                for core in range(2):
                    to = [z, y, x, core]
                    to[axis] = (to[axis] + shift) % sizes[axis]
                    pairs.append((device_of(z, y, x, core), device_of(*to)))
    return lax.ppermute(value, ("grp", "dev"), pairs)


def on_device(x, gate, b, c, decay, d_skip, norm_gain):
    z, r = lax.axis_index("grp"), lax.axis_index("dev")
    place = jnp.stack([z, r // 8, (r // 2) % 4, r % 2]).astype(jnp.int32)
    piece, chunk = (QUARTER + 8, HALF), (QUARTER, HALF)

    keep, send = end_state(place, x, b, decay)
    recv = moved(send, CORE, 1)
    left, b_t, factors = prepare(b, c, decay)
    parts = []

    def work(count, *arrived):
        for _ in range(count):
            parts.append(local(len(parts), d_skip, x, gate, left, b_t, factors))
        arrived, parts[-count:] = lax.optimization_barrier((arrived, parts[-count:]))
        return arrived

    (recv,), (left, b_t, factors) = lax.optimization_barrier(((recv,), (left, b_t, factors)))
    u0, *sends = small_call(pair_kernel, "pair", place, (keep, recv), [piece] * 4)
    lines = [u0] + list(work(1, *[moved(v, X, s + 1) for s, v in enumerate(sends)]))
    (v0,) = small_call(line_kernel, "line", place, lines, [piece])
    columns = [v0] + list(work(2, *[moved(v0, Y, s) for s in (1, 2, 3)]))
    w0, before = small_call(plane_kernel, "plane", place, columns, [piece] * 2)
    planes = [w0] + list(work(2, *[moved(w0, Z, s) for s in (1, 2, 3)]))
    e0, *sends = small_call(enter_kernel, "enter", place, planes + [before] + lines, [chunk] * 4)
    entering = [e0] + list(work(1, *[moved(v, X, s + 1) for s, v in enumerate(sends)]))
    own, send = small_call(chip_kernel, "chip", place, entering + [keep, recv], [(STATE, HALF)] * 2)
    other = moved(send, CORE, 1)
    sums, weights = zip(*parts, strict=True)
    return output(place, c, norm_gain[None], own, other, sums, weights)


def solution(mesh):
    return jax.shard_map(
        on_device,
        mesh=mesh,
        in_specs=(
            P(("grp", "dev"), None),
            P(("grp", "dev"), None),
            P(("grp", "dev"), None),
            P(("grp", "dev"), None),
            P(None, ("grp", "dev")),
            P(),
            P(),
        ),
        out_specs=P(("grp", "dev"), None),
        check_vma=False,
    )
```

```python
import functools

import jax
import jax.numpy as jnp
from jax import lax
from jax.experimental import pallas as pl
from jax.experimental.pallas import tpu as pltpu
from jax.sharding import PartitionSpec as P

HEADS = 24
HEAD = 64
STATE = 128
WIDTH = HEADS * HEAD
HALF = WIDTH // 2
SUB = 128
STEP = 256
GROUP = 256
ROWS = STATE + 8
SHIFT = 74
SHIFT_LOG = 51.29289136
OUT_STEP = 256
QUARTER = STATE // 4
FIRST_LIMIT = 42 * 1024 * 1024
PREPARE_LIMIT = 40 * 1024 * 1024
LIMIT = 18 * 1024 * 1024
SMALL_LIMIT = 6 * 1024 * 1024
F32 = jnp.float32
BF16 = jnp.bfloat16


def dot(a, b, dims=((1,), (0,))):
    return lax.dot_general(a, b, (dims, ((), ())), preferred_element_type=F32)


def iota(shape, dim):
    return lax.broadcasted_iota(jnp.int32, shape, dim)


def three(v):
    high = v.astype(BF16)
    rest = v - high.astype(F32)
    middle = rest.astype(BF16)
    low = (rest - middle.astype(F32)).astype(BF16)
    return high, middle, low


def spread_parts(v):
    high, middle, low = three(v)
    lane = iota(v.shape, 1)
    picked = jnp.where(
        lane < HEADS, high.astype(F32), jnp.where(lane < 2 * HEADS, middle.astype(F32), low.astype(F32))
    )
    return picked.astype(BF16)


def decay_sums(matrix, decay):
    high, middle, low = three(decay)
    nt = ((1,), (1,))
    return dot(matrix, high, nt) + (dot(matrix, middle, nt) + dot(matrix, low, nt))


def spread_matrix(start, width):
    k, lane = iota((3 * HEADS, width), 0), start + iota((3 * HEADS, width), 1)
    return jnp.where(k % HEADS == lane // HEAD, 1.0, 0.0).astype(BF16)


def half_state(x, b, factors, scaled, start, out, fetched):
    lanes = pl.ds(pl.multiple_of(start, HALF), HALF)
    spread = spread_matrix(start, HALF)
    tokens = x.shape[0]
    for i in range(tokens // STEP):
        fetched(i)
        rows = slice(i * STEP, (i + 1) * STEP)
        scaled[rows] = (x[rows, lanes].astype(F32) * dot(factors[rows], spread)).astype(BF16)
    fetched(tokens // STEP)
    out[:STATE] = dot(b[...], scaled[...], ((0,), (0,)))
    out[STATE:] = dot(factors[tokens:], spread)[:8]


def send_state_kernel(place, x_hbm, b_hbm, decay_hbm, send_ref, x, b, factors, decay, scaled, sems):
    tokens = x.shape[0]
    steps = tokens // STEP
    fetch_decay = pltpu.make_async_copy(decay_hbm, decay, sems.at[steps + 1])
    fetch_decay.start()
    copies = []
    for i in range(steps):
        rows = pl.ds(i * STEP, STEP)
        copies.append(pltpu.make_async_copy(x_hbm.at[rows], x.at[rows], sems.at[i]))
    copies.append(pltpu.make_async_copy(b_hbm, b, sems.at[steps]))
    for copy in copies:
        copy.start()
    row, col = iota((STEP + 16, STEP), 0), iota((STEP + 16, STEP), 1)
    later = jnp.where((col > row) | (row >= STEP), 1.0, 0.0).astype(BF16)
    fetch_decay.wait()
    sums = []
    for i in range(steps):
        part = decay[:, i * STEP : (i + 1) * STEP]
        sums.append(decay_sums(later, jnp.concatenate([part] * 3, axis=0)))
    after = jnp.zeros((1, 3 * HEADS), F32)
    for i in reversed(range(steps)):
        factors[i * STEP : (i + 1) * STEP] = spread_parts(jnp.exp(sums[i][:STEP] + after))
        after = after + sums[i][STEP : STEP + 1]
    factors[tokens:] = spread_parts(jnp.exp(jnp.broadcast_to(after, (16, 3 * HEADS))))
    half_state(x, b, factors, scaled, (1 - place[CORE]) * HALF, send_ref, lambda i: copies[i].wait())


def send_state(place, x, b, decay):
    tokens = x.shape[0]
    vmem = pl.BlockSpec(memory_space=pltpu.VMEM)
    return pl.pallas_call(
        send_state_kernel,
        in_specs=[pl.BlockSpec(memory_space=pltpu.SMEM)] + [pl.BlockSpec(memory_space=pltpu.HBM)] * 3,
        out_specs=[vmem] * 4,
        out_shape=[
            jax.ShapeDtypeStruct((ROWS, HALF), F32),
            jax.ShapeDtypeStruct(x.shape, BF16),
            jax.ShapeDtypeStruct(b.shape, BF16),
            jax.ShapeDtypeStruct((tokens + 16, 3 * HEADS), BF16),
        ],
        scratch_shapes=[
            pltpu.VMEM(decay.shape, F32),
            pltpu.VMEM((tokens, HALF), BF16),
            pltpu.SemaphoreType.DMA((tokens // STEP + 2,)),
        ],
        name="send_state",
        compiler_params=pltpu.CompilerParams(vmem_limit_bytes=FIRST_LIMIT),
    )(place, x, b, decay)


def keep_state_kernel(place, x, b, factors, keep_ref, scaled):
    half_state(x, b, factors, scaled, place[CORE] * HALF, keep_ref, lambda i: None)


def keep_state(place, x, b, factors):
    vmem = pl.BlockSpec(memory_space=pltpu.VMEM)
    return pl.pallas_call(
        keep_state_kernel,
        in_specs=[pl.BlockSpec(memory_space=pltpu.SMEM)] + [vmem] * 3,
        out_specs=vmem,
        out_shape=jax.ShapeDtypeStruct((ROWS, HALF), F32),
        scratch_shapes=[pltpu.VMEM((x.shape[0], HALF), BF16)],
        name="keep_state",
        compiler_params=pltpu.CompilerParams(vmem_limit_bytes=LIMIT),
    )(place, x, b, factors)


def small_call(kernel, name, place, args, outs):
    vmem = pl.BlockSpec(memory_space=pltpu.VMEM)
    return pl.pallas_call(
        kernel,
        in_specs=[pl.BlockSpec(memory_space=pltpu.SMEM)] + [vmem] * len(args),
        out_specs=[vmem] * len(outs),
        out_shape=[jax.ShapeDtypeStruct(s, F32) for s in outs],
        name=name,
        compiler_params=pltpu.CompilerParams(vmem_limit_bytes=SMALL_LIMIT),
    )(place, *args)


Z, Y, X, CORE = 0, 1, 2, 3


def pair_kernel(place, keep, recv, own, *sends):
    flip = place[CORE] == 1
    kept, got = keep[STATE : STATE + 8], recv[STATE : STATE + 8]
    late = jnp.where(flip, kept, got)[:1]
    decay = kept * got
    for shift, out in enumerate((own,) + sends):
        chunk = (place[X] + shift) % 4
        rows = pl.ds(pl.multiple_of(chunk * QUARTER, QUARTER), QUARTER)
        a, b = keep[rows], recv[rows]
        out[:QUARTER] = late * jnp.where(flip, b, a) + jnp.where(flip, a, b)
        out[QUARTER:] = decay


def ordered(place, axis, refs, j):
    shift = (place[axis] - j + 4) % 4
    value = refs[0][...]
    for s in (1, 2, 3):
        value = jnp.where(shift == s, refs[s][...], value)
    return value


def line_kernel(place, u0, u1, u2, u3, total):
    state = jnp.zeros((QUARTER, HALF), F32)
    decay = jnp.ones((8, HALF), F32)
    for j in range(4):
        u = ordered(place, X, (u0, u1, u2, u3), j)
        state = u[QUARTER : QUARTER + 1] * state + u[:QUARTER]
        decay = decay * u[QUARTER:]
    total[:QUARTER] = state
    total[QUARTER:] = decay


def plane_kernel(place, v0, v1, v2, v3, total, before):
    state = jnp.zeros((QUARTER, HALF), F32)
    decay = jnp.ones((8, HALF), F32)
    for j in range(4):

        @pl.when(place[Y] == j)
        def _(state=state, decay=decay):
            before[:QUARTER] = state
            before[QUARTER:] = decay

        v = ordered(place, Y, (v0, v1, v2, v3), j)
        state = v[QUARTER : QUARTER + 1] * state + v[:QUARTER]
        decay = decay * v[QUARTER:]
    total[:QUARTER] = state
    total[QUARTER:] = decay


def enter_kernel(place, w0, w1, w2, w3, before, u0, u1, u2, u3, own, *sends):
    state = jnp.zeros((QUARTER, HALF), F32)
    for j in range(3):
        w = ordered(place, Z, (w0, w1, w2, w3), j)
        updated = w[QUARTER : QUARTER + 1] * state + w[:QUARTER]
        state = jnp.where(j < place[Z], updated, state)
    state = before[QUARTER : QUARTER + 1] * state + before[:QUARTER]
    for j in range(4):
        for shift, out in enumerate((own,) + sends):

            @pl.when((place[X] + shift) % 4 == j)
            def _(state=state, out=out):
                out[...] = state

        if j < 3:
            u = ordered(place, X, (u0, u1, u2, u3), j)
            state = u[QUARTER : QUARTER + 1] * state + u[:QUARTER]


def chip_kernel(place, e0, e1, e2, e3, keep, recv, own, send):
    flip = place[CORE] == 1
    first = jnp.where(flip, recv[STATE : STATE + 1], keep[STATE : STATE + 1])
    for shift, e in enumerate((e0, e1, e2, e3)):
        chunk = (place[X] - shift + 4) % 4
        rows = pl.ds(pl.multiple_of(chunk * QUARTER, QUARTER), QUARTER)
        at_first = e[...]
        at_second = first * at_first + jnp.where(flip, recv[rows], keep[rows])
        own[rows] = jnp.where(flip, at_second, at_first)
        send[rows] = jnp.where(flip, at_first, at_second)


BEFORE = SUB + 16
AFTER = 2 * SUB


def prepare_kernel(gate_hbm, b_ref, c_ref, decay_ref, gate, left_ref, b_t_ref, before_ref, after_ref, sem):
    fetch = pltpu.make_async_copy(gate_hbm, gate, sem)
    fetch.start()
    tokens = b_ref.shape[0]
    row, col = iota((SUB, SUB), 0), iota((SUB, SUB), 1)
    causal = col <= row
    upto = jnp.where(causal, 1.0, 0.0).astype(BF16)
    start = jnp.zeros((1, 3 * HEADS), F32)
    for s in range(tokens // SUB):
        rows = slice(s * SUB, (s + 1) * SUB)
        decay = decay_ref[:, rows]
        cumul = decay_sums(upto, jnp.concatenate([decay] * 3, axis=0))
        end = cumul[SUB - 1 : SUB]
        shifted = end + SHIFT_LOG
        exponents = [shifted - cumul, jnp.broadcast_to(shifted, (16, 3 * HEADS)), cumul - shifted, cumul + start]
        factors = spread_parts(jnp.exp(jnp.concatenate(exponents, axis=0)))
        before_ref[s * BEFORE : (s + 1) * BEFORE] = factors[:BEFORE]
        after_ref[s * AFTER : (s + 1) * AFTER] = factors[BEFORE:]
        start = start + end
        b, c = b_ref[rows], c_ref[rows]
        scores = jnp.where(causal, dot(c, b, ((1,), (1,))), 0.0)
        left_ref[rows, :SUB] = scores.astype(BF16)
        left_ref[rows, SUB:] = c
        b_t_ref[rows] = jnp.transpose(b.astype(F32)).astype(BF16)
    fetch.wait()


def prepare(gate, b, c, decay):
    tokens = b.shape[0]
    subs = tokens // SUB
    vmem = pl.BlockSpec(memory_space=pltpu.VMEM)
    return pl.pallas_call(
        prepare_kernel,
        in_specs=[pl.BlockSpec(memory_space=pltpu.HBM)] + [vmem] * 3,
        out_specs=[vmem] * 5,
        out_shape=[
            jax.ShapeDtypeStruct(gate.shape, BF16),
            jax.ShapeDtypeStruct((tokens, SUB + STATE), BF16),
            jax.ShapeDtypeStruct((tokens, SUB), BF16),
            jax.ShapeDtypeStruct((subs * BEFORE, 3 * HEADS), BF16),
            jax.ShapeDtypeStruct((subs * AFTER, 3 * HEADS), BF16),
        ],
        scratch_shapes=[pltpu.SemaphoreType.DMA],
        name="prepare",
        compiler_params=pltpu.CompilerParams(vmem_limit_bytes=PREPARE_LIMIT),
    )(gate, b, c, decay)


def local_kernel(
    part, place, skip_ref, x_ref, gate_ref, left_ref, b_t_ref, before_ref, after_ref, sum_ref, weight_ref,
    scaled, carried,
):
    tokens = x_ref.shape[0]
    group = lax.rem(place[CORE] * (HALF // GROUP) + part, WIDTH // GROUP)
    start = pl.multiple_of(group * GROUP, GROUP)
    lanes = pl.ds(start, GROUP)
    spread = spread_matrix(start, GROUP)
    lane = iota((1, GROUP), 1)
    skip = jnp.zeros((1, GROUP), F32)
    for h in range(GROUP // HEAD):
        skip = jnp.where(lane // HEAD == h, skip_ref[group * (GROUP // HEAD) + h], skip)
    state = jnp.zeros((STATE, GROUP), F32)
    down = 2.0**-SHIFT
    before = dot(before_ref[...], spread)
    for s in range(tokens // SUB):
        rows = slice(s * SUB, (s + 1) * SUB)
        wide = before[s * BEFORE : (s + 1) * BEFORE]
        scaled[rows] = (x_ref[rows, lanes].astype(F32) * wide[:SUB]).astype(BF16)
        decayed = state * wide[SUB : SUB + 1]
        carried[rows] = decayed.astype(BF16)
        state = (decayed + dot(b_t_ref[rows], scaled[rows])) * down
    after = dot(after_ref[...], spread)
    for s in range(tokens // SUB):
        rows = slice(s * SUB, (s + 1) * SUB)
        wide = after[s * AFTER : (s + 1) * AFTER]
        own = dot(left_ref[rows], jnp.concatenate([scaled[rows], carried[rows]], axis=0))
        summed = own * wide[:SUB] + skip * x_ref[rows, lanes].astype(F32)
        h = 0.5 * gate_ref[rows, lanes].astype(F32)
        silu = h + h * jnp.tanh(h)
        sum_ref[rows] = summed * silu
        weight_ref[rows] = (wide[SUB:] * silu).astype(BF16)


def local(part, place, skip, x, gate, left, b_t, before, after):
    tokens = x.shape[0]
    vmem = pl.BlockSpec(memory_space=pltpu.VMEM)
    return pl.pallas_call(
        functools.partial(local_kernel, part),
        in_specs=[pl.BlockSpec(memory_space=pltpu.SMEM)] * 2 + [vmem] * 6,
        out_specs=[vmem] * 2,
        out_shape=[jax.ShapeDtypeStruct((tokens, GROUP), F32), jax.ShapeDtypeStruct((tokens, GROUP), BF16)],
        scratch_shapes=[pltpu.VMEM((tokens, GROUP), BF16)] * 2,
        name="local",
        compiler_params=pltpu.CompilerParams(vmem_limit_bytes=LIMIT),
    )(place, skip, x, gate, left, b_t, before, after)


def output_kernel(mine, place, c_ref, gain_ref, state_ref, *refs):
    groups = HALF // GROUP
    sums, weights = refs[:groups], refs[groups : 2 * groups]
    out_hbm, state, out, sems = refs[-4:]
    state[...] = state_ref[...].astype(BF16)
    half = pl.multiple_of((place[CORE] if mine else 1 - place[CORE]) * HALF, HALF)
    same = iota((GROUP, GROUP), 0) // HEAD == iota((GROUP, GROUP), 1) // HEAD
    mean = jnp.where(same, 1.0 / HEAD, 0.0).astype(BF16)
    copies = []
    for i in range(out.shape[0] // OUT_STEP):
        rows = slice(i * OUT_STEP, (i + 1) * OUT_STEP)
        for g in range(groups):
            lanes = slice(g * GROUP, (g + 1) * GROUP)
            gain = gain_ref[:, pl.ds(pl.multiple_of(half + g * GROUP, GROUP), GROUP)]
            entering = dot(c_ref[rows], state[:, lanes])
            gated = sums[g][rows] + weights[g][rows].astype(F32) * entering
            square = dot((gated * gated).astype(BF16), mean)
            out[rows, lanes] = (gated * lax.rsqrt(square + 1e-5) * gain).astype(BF16)
        where = pl.ds(i * OUT_STEP, OUT_STEP)
        copies.append(pltpu.make_async_copy(out.at[where], out_hbm.at[where, pl.ds(half, HALF)], sems.at[i]))
        copies[-1].start()
    for copy in copies:
        copy.wait()


def output(mine, place, c, gain, state, parts, *half_done):
    tokens = c.shape[0]
    sums, weights = zip(*parts, strict=True)
    args = (place, c, gain, state, *sums, *weights)
    vmem = pl.BlockSpec(memory_space=pltpu.VMEM)
    hbm = pl.BlockSpec(memory_space=pl.ANY)
    return pl.pallas_call(
        functools.partial(output_kernel, mine),
        in_specs=[pl.BlockSpec(memory_space=pltpu.SMEM)] + [vmem] * (len(args) - 1) + [hbm] * len(half_done),
        out_specs=hbm,
        out_shape=jax.ShapeDtypeStruct((tokens, WIDTH), BF16),
        input_output_aliases={len(args): 0} if half_done else {},
        scratch_shapes=[
            pltpu.VMEM((STATE, HALF), BF16),
            pltpu.VMEM((tokens, HALF), BF16),
            pltpu.SemaphoreType.DMA((tokens // OUT_STEP,)),
        ],
        name="output",
        compiler_params=pltpu.CompilerParams(vmem_limit_bytes=LIMIT),
    )(*args, *half_done)


def device_of(z, y, x, core):
    return ((z * 4 + y) * 4 + x) * 2 + core


def moved(value, axis, shift):
    sizes = (4, 4, 4, 2)
    pairs = []
    for z in range(4):
        for y in range(4):
            for x in range(4):
                for core in range(2):
                    to = [z, y, x, core]
                    to[axis] = (to[axis] + shift) % sizes[axis]
                    pairs.append((device_of(z, y, x, core), device_of(*to)))
    return lax.ppermute(value, ("grp", "dev"), pairs)


def on_device(x, gate, b, c, decay, d_skip, norm_gain):
    z, r = lax.axis_index("grp"), lax.axis_index("dev")
    place = jnp.stack([z, r // 8, (r // 2) % 4, r % 2]).astype(jnp.int32)
    piece, chunk = (QUARTER + 8, HALF), (QUARTER, HALF)

    send, x, b, factors = send_state(place, x, b, decay)
    recv = moved(send, CORE, 1)
    keep = keep_state(place, x, b, factors)
    keep, recv = lax.optimization_barrier((keep, recv))
    parts = []

    def work(count, *arrived):
        for _ in range(count):
            parts.append(local(len(parts), place, d_skip, x, *shared))
        arrived, parts[-count:] = lax.optimization_barrier((arrived, parts[-count:]))
        return arrived

    u0, *sends = small_call(pair_kernel, "pair", place, (keep, recv), [piece] * 4)
    shared = prepare(gate, b, c, decay)
    lines = [u0] + list(work(1, *[moved(v, X, s + 1) for s, v in enumerate(sends)]))
    (v0,) = small_call(line_kernel, "line", place, lines, [piece])
    columns = [v0] + list(work(2, *[moved(v0, Y, s) for s in (1, 2, 3)]))
    w0, before = small_call(plane_kernel, "plane", place, columns, [piece] * 2)
    planes = [w0] + list(work(2, *[moved(w0, Z, s) for s in (1, 2, 3)]))
    e0, *sends = small_call(enter_kernel, "enter", place, planes + [before] + lines, [chunk] * 4)
    entering = [e0] + list(work(1, *[moved(v, X, s + 1) for s, v in enumerate(sends)]))
    own, send = small_call(chip_kernel, "chip", place, entering + [keep, recv], [(STATE, HALF)] * 2)
    other = moved(send, CORE, 1)
    half = len(parts) // 2
    gain = norm_gain[None]
    out = output(True, place, c, gain, own, parts[:half])
    out, other = lax.optimization_barrier((out, other))
    return output(False, place, c, gain, other, parts[half:], out)


def solution(mesh):
    return jax.shard_map(
        on_device,
        mesh=mesh,
        in_specs=(
            P(("grp", "dev"), None),
            P(("grp", "dev"), None),
            P(("grp", "dev"), None),
            P(("grp", "dev"), None),
            P(None, ("grp", "dev")),
            P(),
            P(),
        ),
        out_specs=P(("grp", "dev"), None),
        check_vma=False,
    )
```

```python
import functools

import jax
import jax.numpy as jnp
from jax import lax
from jax.experimental import pallas as pl
from jax.experimental.pallas import tpu as pltpu
from jax.sharding import PartitionSpec as P

HEADS = 24
HEAD = 64
STATE = 128
WIDTH = HEADS * HEAD
HALF = WIDTH // 2
SUB = 128
STEP = 256
GROUP = 256
ROWS = STATE + 8
SHIFT = 74
SHIFT_LOG = 51.29289136
OUT_STEP = 256
FETCH = 512
QUARTER = STATE // 4
FETCH_LIMIT = 42 * 1024 * 1024
PREPARE_LIMIT = 40 * 1024 * 1024
LIMIT = 18 * 1024 * 1024
SMALL_LIMIT = 6 * 1024 * 1024
F32 = jnp.float32
BF16 = jnp.bfloat16


def dot(a, b, dims=((1,), (0,))):
    return lax.dot_general(a, b, (dims, ((), ())), preferred_element_type=F32)


def iota(shape, dim):
    return lax.broadcasted_iota(jnp.int32, shape, dim)


def three(v):
    high = v.astype(BF16)
    rest = v - high.astype(F32)
    middle = rest.astype(BF16)
    low = (rest - middle.astype(F32)).astype(BF16)
    return high, middle, low


def spread_parts(v):
    high, middle, low = three(v)
    lane = iota(v.shape, 1)
    picked = jnp.where(
        lane < HEADS, high.astype(F32), jnp.where(lane < 2 * HEADS, middle.astype(F32), low.astype(F32))
    )
    return picked.astype(BF16)


def decay_sums(matrix, decay):
    high, middle, low = three(decay)
    nt = ((1,), (1,))
    return dot(matrix, high, nt) + (dot(matrix, middle, nt) + dot(matrix, low, nt))


def spread_matrix(start, width):
    k, lane = iota((3 * HEADS, width), 0), start + iota((3 * HEADS, width), 1)
    return jnp.where(k % HEADS == lane // HEAD, 1.0, 0.0).astype(BF16)


def half_copies(place, mine, source, target, sems):
    start = pl.multiple_of((place[CORE] if mine else 1 - place[CORE]) * HALF, HALF)
    copies = []
    for i in range(target.shape[0] // FETCH):
        rows = pl.ds(i * FETCH, FETCH)
        copies.append(pltpu.make_async_copy(source.at[rows, pl.ds(start, HALF)], target.at[rows], sems.at[i]))
    return copies


def factors_kernel(place, x_hbm, decay, x_send, x_keep, factors, sems):
    copies = half_copies(place, False, x_hbm, x_send, sems.at[0]) + half_copies(place, True, x_hbm, x_keep, sems.at[1])
    for copy in copies:
        copy.start()
    tokens = decay.shape[1]
    steps = tokens // STEP
    row, col = iota((STEP + 16, STEP), 0), iota((STEP + 16, STEP), 1)
    later = jnp.where((col > row) | (row >= STEP), 1.0, 0.0).astype(BF16)
    sums = []
    for i in range(steps):
        part = decay[:, i * STEP : (i + 1) * STEP]
        sums.append(decay_sums(later, jnp.concatenate([part] * 3, axis=0)))
    after = jnp.zeros((1, 3 * HEADS), F32)
    for i in reversed(range(steps)):
        factors[i * STEP : (i + 1) * STEP] = spread_parts(jnp.exp(sums[i][:STEP] + after))
        after = after + sums[i][STEP : STEP + 1]
    factors[tokens:] = spread_parts(jnp.exp(jnp.broadcast_to(after, (16, 3 * HEADS))))
    for copy in copies:
        copy.wait()


def decay_factors(place, x, decay):
    tokens = x.shape[0]
    vmem = pl.BlockSpec(memory_space=pltpu.VMEM)
    return pl.pallas_call(
        factors_kernel,
        in_specs=[pl.BlockSpec(memory_space=pltpu.SMEM), pl.BlockSpec(memory_space=pl.ANY), vmem],
        out_specs=[vmem] * 3,
        out_shape=[
            jax.ShapeDtypeStruct((tokens, HALF), BF16),
            jax.ShapeDtypeStruct((tokens, HALF), BF16),
            jax.ShapeDtypeStruct((tokens + 16, 3 * HEADS), BF16),
        ],
        scratch_shapes=[pltpu.SemaphoreType.DMA((2, tokens // FETCH))],
        name="decay_factors",
        compiler_params=pltpu.CompilerParams(vmem_limit_bytes=FETCH_LIMIT),
    )(place, x, decay)


def half_state(x, b, factors, scaled, start, out):
    spread = spread_matrix(start, HALF)
    tokens = x.shape[0]
    for i in range(tokens // STEP):
        rows = slice(i * STEP, (i + 1) * STEP)
        scaled[rows] = (x[rows].astype(F32) * dot(factors[rows], spread)).astype(BF16)
    out[:STATE] = dot(b[...], scaled[...], ((0,), (0,)))
    out[STATE:] = dot(factors[tokens:], spread)[:8]


def state_kernel(mine, place, x, b, factors, out, scaled):
    half_state(x, b, factors, scaled, (place[CORE] if mine else 1 - place[CORE]) * HALF, out)


def end_state(mine, place, x, b, factors):
    vmem = pl.BlockSpec(memory_space=pltpu.VMEM)
    return pl.pallas_call(
        functools.partial(state_kernel, mine),
        in_specs=[pl.BlockSpec(memory_space=pltpu.SMEM)] + [vmem] * 3,
        out_specs=vmem,
        out_shape=jax.ShapeDtypeStruct((ROWS, HALF), F32),
        scratch_shapes=[pltpu.VMEM(x.shape, BF16)],
        name="end_state",
        compiler_params=pltpu.CompilerParams(vmem_limit_bytes=LIMIT),
    )(place, x, b, factors)


def small_call(kernel, name, place, args, outs):
    vmem = pl.BlockSpec(memory_space=pltpu.VMEM)
    return pl.pallas_call(
        kernel,
        in_specs=[pl.BlockSpec(memory_space=pltpu.SMEM)] + [vmem] * len(args),
        out_specs=[vmem] * len(outs),
        out_shape=[jax.ShapeDtypeStruct(s, F32) for s in outs],
        name=name,
        compiler_params=pltpu.CompilerParams(vmem_limit_bytes=SMALL_LIMIT),
    )(place, *args)


Z, Y, X, CORE = 0, 1, 2, 3


def pair_kernel(place, keep, recv, own, *sends):
    flip = place[CORE] == 1
    kept, got = keep[STATE : STATE + 8], recv[STATE : STATE + 8]
    late = jnp.where(flip, kept, got)[:1]
    decay = kept * got
    for shift, out in enumerate((own,) + sends):
        chunk = (place[X] + shift) % 4
        rows = pl.ds(pl.multiple_of(chunk * QUARTER, QUARTER), QUARTER)
        a, b = keep[rows], recv[rows]
        out[:QUARTER] = late * jnp.where(flip, b, a) + jnp.where(flip, a, b)
        out[QUARTER:] = decay


def ordered(place, axis, refs, j):
    shift = (place[axis] - j + 4) % 4
    value = refs[0][...]
    for s in (1, 2, 3):
        value = jnp.where(shift == s, refs[s][...], value)
    return value


def line_kernel(place, u0, u1, u2, u3, total):
    state = jnp.zeros((QUARTER, HALF), F32)
    decay = jnp.ones((8, HALF), F32)
    for j in range(4):
        u = ordered(place, X, (u0, u1, u2, u3), j)
        state = u[QUARTER : QUARTER + 1] * state + u[:QUARTER]
        decay = decay * u[QUARTER:]
    total[:QUARTER] = state
    total[QUARTER:] = decay


def plane_kernel(place, v0, v1, v2, v3, total, before):
    state = jnp.zeros((QUARTER, HALF), F32)
    decay = jnp.ones((8, HALF), F32)
    for j in range(4):

        @pl.when(place[Y] == j)
        def _(state=state, decay=decay):
            before[:QUARTER] = state
            before[QUARTER:] = decay

        v = ordered(place, Y, (v0, v1, v2, v3), j)
        state = v[QUARTER : QUARTER + 1] * state + v[:QUARTER]
        decay = decay * v[QUARTER:]
    total[:QUARTER] = state
    total[QUARTER:] = decay


def enter_kernel(place, w0, w1, w2, w3, before, u0, u1, u2, u3, own, *sends):
    state = jnp.zeros((QUARTER, HALF), F32)
    for j in range(3):
        w = ordered(place, Z, (w0, w1, w2, w3), j)
        updated = w[QUARTER : QUARTER + 1] * state + w[:QUARTER]
        state = jnp.where(j < place[Z], updated, state)
    state = before[QUARTER : QUARTER + 1] * state + before[:QUARTER]
    for j in range(4):
        for shift, out in enumerate((own,) + sends):

            @pl.when((place[X] + shift) % 4 == j)
            def _(state=state, out=out):
                out[...] = state

        if j < 3:
            u = ordered(place, X, (u0, u1, u2, u3), j)
            state = u[QUARTER : QUARTER + 1] * state + u[:QUARTER]


def chip_kernel(place, e0, e1, e2, e3, keep, recv, own, send):
    flip = place[CORE] == 1
    first = jnp.where(flip, recv[STATE : STATE + 1], keep[STATE : STATE + 1])
    for shift, e in enumerate((e0, e1, e2, e3)):
        chunk = (place[X] - shift + 4) % 4
        rows = pl.ds(pl.multiple_of(chunk * QUARTER, QUARTER), QUARTER)
        at_first = e[...]
        at_second = first * at_first + jnp.where(flip, recv[rows], keep[rows])
        own[rows] = jnp.where(flip, at_second, at_first)
        send[rows] = jnp.where(flip, at_first, at_second)


BEFORE = SUB + 16


def prepare_kernel(gate_hbm, b_ref, c_ref, decay_ref, gate, left_ref, b_t_ref, before_ref, after_ref, sem):
    fetch = pltpu.make_async_copy(gate_hbm, gate, sem)
    fetch.start()
    tokens = b_ref.shape[0]
    row, col = iota((SUB, SUB), 0), iota((SUB, SUB), 1)
    causal = col <= row
    upto = jnp.where(causal, 1.0, 0.0).astype(BF16)
    start = jnp.zeros((1, 3 * HEADS), F32)
    for s in range(tokens // SUB):
        rows = slice(s * SUB, (s + 1) * SUB)
        decay = decay_ref[:, rows]
        cumul = decay_sums(upto, jnp.concatenate([decay] * 3, axis=0))
        end = cumul[SUB - 1 : SUB]
        shifted = end + SHIFT_LOG
        ends = [jnp.broadcast_to(v, (8, 3 * HEADS)) for v in (shifted, shifted + start)]
        exponents = [shifted - cumul, *ends, cumul - shifted]
        factors = spread_parts(jnp.exp(jnp.concatenate(exponents, axis=0)))
        before_ref[s * BEFORE : (s + 1) * BEFORE] = factors[:BEFORE]
        after_ref[rows] = factors[BEFORE:]
        start = start + end
        b, c = b_ref[rows], c_ref[rows]
        scores = jnp.where(causal, dot(c, b, ((1,), (1,))), 0.0)
        left_ref[rows, :SUB] = scores.astype(BF16)
        left_ref[rows, SUB:] = c
        b_t_ref[rows] = jnp.transpose(b.astype(F32)).astype(BF16)
    fetch.wait()


def prepare(gate, b, c, decay):
    tokens = b.shape[0]
    subs = tokens // SUB
    vmem = pl.BlockSpec(memory_space=pltpu.VMEM)
    return pl.pallas_call(
        prepare_kernel,
        in_specs=[pl.BlockSpec(memory_space=pltpu.HBM)] + [vmem] * 3,
        out_specs=[vmem] * 5,
        out_shape=[
            jax.ShapeDtypeStruct(gate.shape, BF16),
            jax.ShapeDtypeStruct((tokens, SUB + STATE), BF16),
            jax.ShapeDtypeStruct((tokens, SUB), BF16),
            jax.ShapeDtypeStruct((subs * BEFORE, 3 * HEADS), BF16),
            jax.ShapeDtypeStruct((tokens, 3 * HEADS), BF16),
        ],
        scratch_shapes=[pltpu.SemaphoreType.DMA],
        name="prepare",
        compiler_params=pltpu.CompilerParams(vmem_limit_bytes=PREPARE_LIMIT),
    )(gate, b, c, decay)


def local_kernel(
    part, place, skip_ref, x_ref, gate_ref, left_ref, b_t_ref, before_ref, after_ref, sum_ref, weight_ref,
    scaled, carried,
):
    tokens = x_ref.shape[0]
    group = lax.rem(place[CORE] * (HALF // GROUP) + part, WIDTH // GROUP)
    start = pl.multiple_of(group * GROUP, GROUP)
    lanes = pl.ds(start, GROUP)
    at = part % (HALF // GROUP) * GROUP
    x_lanes = slice(at, at + GROUP)
    spread = spread_matrix(start, GROUP)
    lane = iota((1, GROUP), 1)
    skip = jnp.zeros((1, GROUP), F32)
    for h in range(GROUP // HEAD):
        skip = jnp.where(lane // HEAD == h, skip_ref[group * (GROUP // HEAD) + h], skip)
    state = jnp.zeros((STATE, GROUP), F32)
    down = 2.0**-SHIFT
    before = dot(before_ref[...], spread)
    for s in range(tokens // SUB):
        rows = slice(s * SUB, (s + 1) * SUB)
        wide = before[s * BEFORE : (s + 1) * BEFORE]
        scaled[rows] = (x_ref[rows, x_lanes].astype(F32) * wide[:SUB]).astype(BF16)
        decayed = state * wide[SUB : SUB + 1]
        carried[rows] = decayed.astype(BF16)
        state = (decayed + dot(b_t_ref[rows], scaled[rows])) * down
    after = dot(after_ref[...], spread)
    for s in range(tokens // SUB):
        rows = slice(s * SUB, (s + 1) * SUB)
        own = dot(left_ref[rows], jnp.concatenate([scaled[rows], carried[rows]], axis=0))
        h = 0.5 * gate_ref[rows, lanes].astype(F32)
        silu = h + h * jnp.tanh(h)
        factor = after[rows] * silu
        sum_ref[rows] = own * factor + (skip * x_ref[rows, x_lanes].astype(F32)) * silu
        entering = s * BEFORE + SUB + 8
        weight_ref[rows] = (factor * before[entering : entering + 1]).astype(BF16)


def local(part, place, skip, x, gate, left, b_t, before, after):
    tokens = x.shape[0]
    vmem = pl.BlockSpec(memory_space=pltpu.VMEM)
    return pl.pallas_call(
        functools.partial(local_kernel, part),
        in_specs=[pl.BlockSpec(memory_space=pltpu.SMEM)] * 2 + [vmem] * 6,
        out_specs=[vmem] * 2,
        out_shape=[jax.ShapeDtypeStruct((tokens, GROUP), F32), jax.ShapeDtypeStruct((tokens, GROUP), BF16)],
        scratch_shapes=[pltpu.VMEM((tokens, GROUP), BF16)] * 2,
        name="local",
        compiler_params=pltpu.CompilerParams(vmem_limit_bytes=LIMIT),
    )(place, skip, x, gate, left, b_t, before, after)


def finish(start, c_ref, gain_ref, state_ref, sums, weights, out, rows):
    same = iota((GROUP, GROUP), 0) // HEAD == iota((GROUP, GROUP), 1) // HEAD
    mean = jnp.where(same, 1.0 / HEAD, 0.0).astype(BF16)
    for g in range(HALF // GROUP):
        lanes = slice(g * GROUP, (g + 1) * GROUP)
        gain = gain_ref[:, pl.ds(pl.multiple_of(start + g * GROUP, GROUP), GROUP)]
        entering = dot(c_ref[rows], state_ref[:, lanes].astype(BF16))
        gated = sums[g][rows] + weights[g][rows].astype(F32) * entering
        square = dot((gated * gated).astype(BF16), mean)
        out[rows, lanes] = (gated * lax.rsqrt(square + 1e-5) * gain).astype(BF16)


def own_output_kernel(place, c_ref, gain_ref, state_ref, *refs):
    groups = HALF // GROUP
    out = refs[-1]
    start = place[CORE] * HALF
    for i in range(out.shape[0] // OUT_STEP):
        rows = slice(i * OUT_STEP, (i + 1) * OUT_STEP)
        finish(start, c_ref, gain_ref, state_ref, refs[:groups], refs[groups : 2 * groups], out, rows)


def own_output(place, c, gain, state, parts):
    sums, weights = zip(*parts, strict=True)
    args = (place, c, gain, state, *sums, *weights)
    vmem = pl.BlockSpec(memory_space=pltpu.VMEM)
    return pl.pallas_call(
        own_output_kernel,
        in_specs=[pl.BlockSpec(memory_space=pltpu.SMEM)] + [vmem] * (len(args) - 1),
        out_specs=vmem,
        out_shape=jax.ShapeDtypeStruct((c.shape[0], HALF), BF16),
        name="own_output",
        compiler_params=pltpu.CompilerParams(vmem_limit_bytes=LIMIT),
    )(*args)


def output_kernel(place, c_ref, gain_ref, state_ref, own, *refs):
    groups = HALF // GROUP
    out_hbm, out, own_sem, sems = refs[-4:]
    start = (1 - place[CORE]) * HALF
    own_lanes = pl.ds(pl.multiple_of(place[CORE] * HALF, HALF), HALF)
    lanes = pl.ds(pl.multiple_of(start, HALF), HALF)
    copies = [pltpu.make_async_copy(own, out_hbm.at[:, own_lanes], own_sem)]
    copies[0].start()
    for i in range(out.shape[0] // OUT_STEP):
        rows = slice(i * OUT_STEP, (i + 1) * OUT_STEP)
        finish(start, c_ref, gain_ref, state_ref, refs[:groups], refs[groups : 2 * groups], out, rows)
        where = pl.ds(i * OUT_STEP, OUT_STEP)
        copies.append(pltpu.make_async_copy(out.at[where], out_hbm.at[where, lanes], sems.at[i]))
        copies[-1].start()
    for copy in copies:
        copy.wait()


def output(place, c, gain, state, own, parts):
    tokens = c.shape[0]
    sums, weights = zip(*parts, strict=True)
    args = (place, c, gain, state, own, *sums, *weights)
    vmem = pl.BlockSpec(memory_space=pltpu.VMEM)
    return pl.pallas_call(
        output_kernel,
        in_specs=[pl.BlockSpec(memory_space=pltpu.SMEM)] + [vmem] * (len(args) - 1),
        out_specs=pl.BlockSpec(memory_space=pl.ANY),
        out_shape=jax.ShapeDtypeStruct((tokens, WIDTH), BF16),
        scratch_shapes=[
            pltpu.VMEM((tokens, HALF), BF16),
            pltpu.SemaphoreType.DMA,
            pltpu.SemaphoreType.DMA((tokens // OUT_STEP,)),
        ],
        name="output",
        compiler_params=pltpu.CompilerParams(vmem_limit_bytes=LIMIT),
    )(*args)


def device_of(z, y, x, core):
    return ((z * 4 + y) * 4 + x) * 2 + core


def moved(value, axis, shift):
    sizes = (4, 4, 4, 2)
    pairs = []
    for z in range(4):
        for y in range(4):
            for x in range(4):
                for core in range(2):
                    to = [z, y, x, core]
                    to[axis] = (to[axis] + shift) % sizes[axis]
                    pairs.append((device_of(z, y, x, core), device_of(*to)))
    return lax.ppermute(value, ("grp", "dev"), pairs)


def on_device(x, gate, b, c, decay, d_skip, norm_gain):
    z, r = lax.axis_index("grp"), lax.axis_index("dev")
    place = jnp.stack([z, r // 8, (r // 2) % 4, r % 2]).astype(jnp.int32)
    piece, chunk = (QUARTER + 8, HALF), (QUARTER, HALF)

    x_send, x_keep, factors = decay_factors(place, x, decay)
    send = end_state(False, place, x_send, b, factors)
    recv = moved(send, CORE, 1)
    keep = end_state(True, place, x_keep, b, factors)
    keep, recv = lax.optimization_barrier((keep, recv))
    parts = []

    def work(count, *arrived):
        for _ in range(count):
            part = len(parts)
            half = x_keep if part < HALF // GROUP else x_send
            parts.append(local(part, place, d_skip, half, *shared))
        arrived, parts[-count:] = lax.optimization_barrier((arrived, parts[-count:]))
        return arrived

    u0, *sends = small_call(pair_kernel, "pair", place, (keep, recv), [piece] * 4)
    shared = prepare(gate, b, c, decay)
    lines = [u0] + list(work(1, *[moved(v, X, s + 1) for s, v in enumerate(sends)]))
    (v0,) = small_call(line_kernel, "line", place, lines, [piece])
    columns = [v0] + list(work(2, *[moved(v0, Y, s) for s in (1, 2, 3)]))
    w0, before = small_call(plane_kernel, "plane", place, columns, [piece] * 2)
    planes = [w0] + list(work(2, *[moved(w0, Z, s) for s in (1, 2, 3)]))
    e0, *sends = small_call(enter_kernel, "enter", place, planes + [before] + lines, [chunk] * 4)
    entering = [e0] + list(work(1, *[moved(v, X, s + 1) for s, v in enumerate(sends)]))
    own, send = small_call(chip_kernel, "chip", place, entering + [keep, recv], [(STATE, HALF)] * 2)
    other = moved(send, CORE, 1)
    half = len(parts) // 2
    gain = norm_gain[None]
    own = own_output(place, c, gain, own, parts[:half])
    own, other = lax.optimization_barrier((own, other))
    return output(place, c, gain, other, own, parts[half:])


def solution(mesh):
    return jax.shard_map(
        on_device,
        mesh=mesh,
        in_specs=(
            P(("grp", "dev"), None),
            P(("grp", "dev"), None),
            P(("grp", "dev"), None),
            P(("grp", "dev"), None),
            P(None, ("grp", "dev")),
            P(),
            P(),
        ),
        out_specs=P(("grp", "dev"), None),
        check_vma=False,
    )
```

```python
import functools

import jax
import jax.numpy as jnp
from jax import lax
from jax.experimental import pallas as pl
from jax.experimental.pallas import tpu as pltpu
from jax.sharding import PartitionSpec as P

HEADS = 24
HEAD = 64
STATE = 128
WIDTH = HEADS * HEAD
HALF = WIDTH // 2
SUB = 128
STEP = 256
GROUP = 256
ROWS = STATE + 8
SHIFT = 74
SHIFT_LOG = 51.29289136
OUT_STEP = 256
FETCH = 512
QUARTER = STATE // 4
TILES = QUARTER // 8 * (HALF // 128)
FETCH_LIMIT = 42 * 1024 * 1024
PREPARE_LIMIT = 40 * 1024 * 1024
LIMIT = 18 * 1024 * 1024
SMALL_LIMIT = 6 * 1024 * 1024
F32 = jnp.float32
BF16 = jnp.bfloat16


def dot(a, b, dims=((1,), (0,))):
    return lax.dot_general(a, b, (dims, ((), ())), preferred_element_type=F32)


def iota(shape, dim):
    return lax.broadcasted_iota(jnp.int32, shape, dim)


def three(v):
    high = v.astype(BF16)
    rest = v - high.astype(F32)
    middle = rest.astype(BF16)
    low = (rest - middle.astype(F32)).astype(BF16)
    return high, middle, low


def spread_parts(v):
    high, middle, low = three(v)
    lane = iota(v.shape, 1)
    picked = jnp.where(
        lane < HEADS, high.astype(F32), jnp.where(lane < 2 * HEADS, middle.astype(F32), low.astype(F32))
    )
    return picked.astype(BF16)


def decay_sums(matrix, decay):
    high, middle, low = three(decay)
    nt = ((1,), (1,))
    return dot(matrix, high, nt) + (dot(matrix, middle, nt) + dot(matrix, low, nt))


def spread_matrix(start, width):
    k, lane = iota((3 * HEADS, width), 0), start + iota((3 * HEADS, width), 1)
    return jnp.where(k % HEADS == lane // HEAD, 1.0, 0.0).astype(BF16)


def half_copies(place, mine, source, target, sems):
    start = pl.multiple_of((place[CORE] if mine else 1 - place[CORE]) * HALF, HALF)
    copies = []
    for i in range(target.shape[0] // FETCH):
        rows = pl.ds(i * FETCH, FETCH)
        copies.append(pltpu.make_async_copy(source.at[rows, pl.ds(start, HALF)], target.at[rows], sems.at[i]))
    return copies


def factors_kernel(place, x_hbm, decay, x_send, x_keep, factors, sems):
    copies = half_copies(place, False, x_hbm, x_send, sems.at[0]) + half_copies(place, True, x_hbm, x_keep, sems.at[1])
    for copy in copies:
        copy.start()
    tokens = decay.shape[1]
    steps = tokens // STEP
    row, col = iota((STEP + 16, STEP), 0), iota((STEP + 16, STEP), 1)
    later = jnp.where((col > row) | (row >= STEP), 1.0, 0.0).astype(BF16)
    sums = []
    for i in range(steps):
        part = decay[:, i * STEP : (i + 1) * STEP]
        sums.append(decay_sums(later, jnp.concatenate([part] * 3, axis=0)))
    after = jnp.zeros((1, 3 * HEADS), F32)
    for i in reversed(range(steps)):
        factors[i * STEP : (i + 1) * STEP] = spread_parts(jnp.exp(sums[i][:STEP] + after))
        after = after + sums[i][STEP : STEP + 1]
    factors[tokens:] = spread_parts(jnp.exp(jnp.broadcast_to(after, (16, 3 * HEADS))))
    for copy in copies:
        copy.wait()


def decay_factors(place, x, decay):
    tokens = x.shape[0]
    vmem = pl.BlockSpec(memory_space=pltpu.VMEM)
    return pl.pallas_call(
        factors_kernel,
        in_specs=[pl.BlockSpec(memory_space=pltpu.SMEM), pl.BlockSpec(memory_space=pl.ANY), vmem],
        out_specs=[vmem] * 3,
        out_shape=[
            jax.ShapeDtypeStruct((tokens, HALF), BF16),
            jax.ShapeDtypeStruct((tokens, HALF), BF16),
            jax.ShapeDtypeStruct((tokens + 16, 3 * HEADS), BF16),
        ],
        scratch_shapes=[pltpu.SemaphoreType.DMA((2, tokens // FETCH))],
        name="decay_factors",
        compiler_params=pltpu.CompilerParams(vmem_limit_bytes=FETCH_LIMIT),
    )(place, x, decay)


def half_state(x, b, factors, scaled, start, out):
    spread = spread_matrix(start, HALF)
    tokens = x.shape[0]
    for i in range(tokens // STEP):
        rows = slice(i * STEP, (i + 1) * STEP)
        scaled[rows] = (x[rows].astype(F32) * dot(factors[rows], spread)).astype(BF16)
    out[:STATE] = dot(b[...], scaled[...], ((0,), (0,)))
    out[STATE:] = dot(factors[tokens:], spread)[:8]


def state_kernel(mine, place, x, b, factors, out, scaled):
    half_state(x, b, factors, scaled, (place[CORE] if mine else 1 - place[CORE]) * HALF, out)


def end_state(mine, place, x, b, factors):
    vmem = pl.BlockSpec(memory_space=pltpu.VMEM)
    return pl.pallas_call(
        functools.partial(state_kernel, mine),
        in_specs=[pl.BlockSpec(memory_space=pltpu.SMEM)] + [vmem] * 3,
        out_specs=vmem,
        out_shape=jax.ShapeDtypeStruct((ROWS, HALF), F32),
        scratch_shapes=[pltpu.VMEM(x.shape, BF16)],
        name="end_state",
        compiler_params=pltpu.CompilerParams(vmem_limit_bytes=LIMIT),
    )(place, x, b, factors)


def small_call(kernel, name, place, args, outs):
    vmem = pl.BlockSpec(memory_space=pltpu.VMEM)
    return pl.pallas_call(
        kernel,
        in_specs=[pl.BlockSpec(memory_space=pltpu.SMEM)] + [vmem] * len(args),
        out_specs=[vmem] * len(outs),
        out_shape=[jax.ShapeDtypeStruct(s, F32) for s in outs],
        name=name,
        compiler_params=pltpu.CompilerParams(vmem_limit_bytes=SMALL_LIMIT),
    )(place, *args)


Z, Y, X, CORE = 0, 1, 2, 3


def parts_of(piece):
    state = piece[:TILES].reshape(QUARTER // 8, HALF // 128, 8, 128)
    decay = [jnp.broadcast_to(piece[TILES, j : j + 1], (8, 128)) for j in range(HALF // 128)]
    return state, jnp.stack(decay)


def set_piece(out, state, decay):
    out[:TILES] = state.reshape(TILES, 8, 128)
    out[TILES] = jnp.zeros((8, 128), F32)
    for j in range(HALF // 128):
        out[TILES, j : j + 1] = decay[j, :1]


def nothing():
    return jnp.zeros((QUARTER // 8, HALF // 128, 8, 128), F32), jnp.ones((HALF // 128, 8, 128), F32)


def pair_kernel(place, keep, recv, own, *sends):
    flip = place[CORE] == 1
    kept, got = keep[STATE : STATE + 8], recv[STATE : STATE + 8]
    late = jnp.where(flip, kept, got)[:1]
    decay = kept * got
    for shift, out in enumerate((own,) + sends):
        chunk = (place[X] + shift) % 4
        rows = pl.ds(pl.multiple_of(chunk * QUARTER, QUARTER), QUARTER)
        a, b = keep[rows], recv[rows]
        total = late * jnp.where(flip, b, a) + jnp.where(flip, a, b)
        out[TILES] = jnp.zeros((8, 128), F32)
        for j in range(HALF // 128):
            lanes = slice(128 * j, 128 * (j + 1))
            out[TILES, j : j + 1] = decay[:1, lanes]
            for i in range(QUARTER // 8):
                out[i * (HALF // 128) + j] = total[8 * i : 8 * (i + 1), lanes]


def ordered(place, axis, refs, j):
    shift = (place[axis] - j + 4) % 4
    value = refs[0][...]
    for s in (1, 2, 3):
        value = jnp.where(shift == s, refs[s][...], value)
    return parts_of(value)


def line_kernel(place, u0, u1, u2, u3, total):
    state, decay = nothing()
    for j in range(4):
        u, u_decay = ordered(place, X, (u0, u1, u2, u3), j)
        state = u_decay * state + u
        decay = decay * u_decay
    set_piece(total, state, decay)


def plane_kernel(place, v0, v1, v2, v3, total, before):
    state, decay = nothing()
    for j in range(4):

        @pl.when(place[Y] == j)
        def _(state=state, decay=decay):
            set_piece(before, state, decay)

        v, v_decay = ordered(place, Y, (v0, v1, v2, v3), j)
        state = v_decay * state + v
        decay = decay * v_decay
    set_piece(total, state, decay)


def enter_kernel(place, w0, w1, w2, w3, before, u0, u1, u2, u3, own, *sends):
    state, _ = nothing()
    for j in range(3):
        w, w_decay = ordered(place, Z, (w0, w1, w2, w3), j)
        state = jnp.where(j < place[Z], w_decay * state + w, state)
    earlier, decay = parts_of(before[...])
    state = decay * state + earlier
    for j in range(4):
        for shift, out in enumerate((own,) + sends):

            @pl.when((place[X] + shift) % 4 == j)
            def _(state=state, out=out):
                for a in range(QUARTER // 8):
                    for b in range(HALF // 128):
                        out[8 * a : 8 * (a + 1), 128 * b : 128 * (b + 1)] = state[a, b]

        if j < 3:
            u, u_decay = ordered(place, X, (u0, u1, u2, u3), j)
            state = u_decay * state + u


def chip_kernel(place, e0, e1, e2, e3, keep, recv, own, send):
    flip = place[CORE] == 1
    first = jnp.where(flip, recv[STATE : STATE + 1], keep[STATE : STATE + 1])
    for shift, e in enumerate((e0, e1, e2, e3)):
        chunk = (place[X] - shift + 4) % 4
        rows = pl.ds(pl.multiple_of(chunk * QUARTER, QUARTER), QUARTER)
        at_first = e[...]
        at_second = first * at_first + jnp.where(flip, recv[rows], keep[rows])
        own[rows] = jnp.where(flip, at_second, at_first)
        send[rows] = jnp.where(flip, at_first, at_second)


BEFORE = SUB + 16


def prepare_kernel(gate_hbm, b_ref, c_ref, decay_ref, gate, left_ref, b_t_ref, before_ref, after_ref, sem):
    fetch = pltpu.make_async_copy(gate_hbm, gate, sem)
    fetch.start()
    tokens = b_ref.shape[0]
    row, col = iota((SUB, SUB), 0), iota((SUB, SUB), 1)
    causal = col <= row
    upto = jnp.where(causal, 1.0, 0.0).astype(BF16)
    start = jnp.zeros((1, 3 * HEADS), F32)
    for s in range(tokens // SUB):
        rows = slice(s * SUB, (s + 1) * SUB)
        decay = decay_ref[:, rows]
        cumul = decay_sums(upto, jnp.concatenate([decay] * 3, axis=0))
        end = cumul[SUB - 1 : SUB]
        shifted = end + SHIFT_LOG
        ends = [jnp.broadcast_to(v, (8, 3 * HEADS)) for v in (shifted, shifted + start)]
        exponents = [shifted - cumul, *ends, cumul - shifted]
        factors = spread_parts(jnp.exp(jnp.concatenate(exponents, axis=0)))
        before_ref[s * BEFORE : (s + 1) * BEFORE] = factors[:BEFORE]
        after_ref[rows] = factors[BEFORE:]
        start = start + end
        b, c = b_ref[rows], c_ref[rows]
        scores = jnp.where(causal, dot(c, b, ((1,), (1,))), 0.0)
        left_ref[rows, :SUB] = scores.astype(BF16)
        left_ref[rows, SUB:] = c
        b_t_ref[rows] = jnp.transpose(b.astype(F32)).astype(BF16)
    fetch.wait()


def prepare(gate, b, c, decay):
    tokens = b.shape[0]
    subs = tokens // SUB
    vmem = pl.BlockSpec(memory_space=pltpu.VMEM)
    return pl.pallas_call(
        prepare_kernel,
        in_specs=[pl.BlockSpec(memory_space=pltpu.HBM)] + [vmem] * 3,
        out_specs=[vmem] * 5,
        out_shape=[
            jax.ShapeDtypeStruct(gate.shape, BF16),
            jax.ShapeDtypeStruct((tokens, SUB + STATE), BF16),
            jax.ShapeDtypeStruct((tokens, SUB), BF16),
            jax.ShapeDtypeStruct((subs * BEFORE, 3 * HEADS), BF16),
            jax.ShapeDtypeStruct((tokens, 3 * HEADS), BF16),
        ],
        scratch_shapes=[pltpu.SemaphoreType.DMA],
        name="prepare",
        compiler_params=pltpu.CompilerParams(vmem_limit_bytes=PREPARE_LIMIT),
    )(gate, b, c, decay)


def local_kernel(
    part, place, skip_ref, x_ref, gate_ref, left_ref, b_t_ref, before_ref, after_ref, sum_ref, weight_ref,
    scaled, carried,
):
    tokens = x_ref.shape[0]
    group = lax.rem(place[CORE] * (HALF // GROUP) + part, WIDTH // GROUP)
    start = pl.multiple_of(group * GROUP, GROUP)
    lanes = pl.ds(start, GROUP)
    at = part % (HALF // GROUP) * GROUP
    x_lanes = slice(at, at + GROUP)
    spread = spread_matrix(start, GROUP)
    lane = iota((1, GROUP), 1)
    skip = jnp.zeros((1, GROUP), F32)
    for h in range(GROUP // HEAD):
        skip = jnp.where(lane // HEAD == h, skip_ref[group * (GROUP // HEAD) + h], skip)
    state = jnp.zeros((STATE, GROUP), F32)
    down = 2.0**-SHIFT
    before = dot(before_ref[...], spread)
    for s in range(tokens // SUB):
        rows = slice(s * SUB, (s + 1) * SUB)
        wide = before[s * BEFORE : (s + 1) * BEFORE]
        scaled[rows] = (x_ref[rows, x_lanes].astype(F32) * wide[:SUB]).astype(BF16)
        decayed = state * wide[SUB : SUB + 1]
        carried[rows] = decayed.astype(BF16)
        state = (decayed + dot(b_t_ref[rows], scaled[rows])) * down
    after = dot(after_ref[...], spread)
    for s in range(tokens // SUB):
        rows = slice(s * SUB, (s + 1) * SUB)
        own = dot(left_ref[rows], jnp.concatenate([scaled[rows], carried[rows]], axis=0))
        h = 0.5 * gate_ref[rows, lanes].astype(F32)
        silu = h + h * jnp.tanh(h)
        factor = after[rows] * silu
        sum_ref[rows] = own * factor + (skip * x_ref[rows, x_lanes].astype(F32)) * silu
        entering = s * BEFORE + SUB + 8
        weight_ref[rows] = (factor * before[entering : entering + 1]).astype(BF16)


def local(part, place, skip, x, gate, left, b_t, before, after):
    tokens = x.shape[0]
    vmem = pl.BlockSpec(memory_space=pltpu.VMEM)
    return pl.pallas_call(
        functools.partial(local_kernel, part),
        in_specs=[pl.BlockSpec(memory_space=pltpu.SMEM)] * 2 + [vmem] * 6,
        out_specs=[vmem] * 2,
        out_shape=[jax.ShapeDtypeStruct((tokens, GROUP), F32), jax.ShapeDtypeStruct((tokens, GROUP), BF16)],
        scratch_shapes=[pltpu.VMEM((tokens, GROUP), BF16)] * 2,
        name="local",
        compiler_params=pltpu.CompilerParams(vmem_limit_bytes=LIMIT),
    )(place, skip, x, gate, left, b_t, before, after)


def finish(start, c_ref, gain_ref, state_ref, sums, weights, out, rows):
    same = iota((GROUP, GROUP), 0) // HEAD == iota((GROUP, GROUP), 1) // HEAD
    mean = jnp.where(same, 1.0 / HEAD, 0.0).astype(BF16)
    for g in range(HALF // GROUP):
        lanes = slice(g * GROUP, (g + 1) * GROUP)
        gain = gain_ref[:, pl.ds(pl.multiple_of(start + g * GROUP, GROUP), GROUP)]
        entering = dot(c_ref[rows], state_ref[:, lanes].astype(BF16))
        gated = sums[g][rows] + weights[g][rows].astype(F32) * entering
        square = dot((gated * gated).astype(BF16), mean)
        out[rows, lanes] = (gated * lax.rsqrt(square + 1e-5) * gain).astype(BF16)


def own_output_kernel(place, c_ref, gain_ref, state_ref, *refs):
    groups = HALF // GROUP
    out = refs[-1]
    start = place[CORE] * HALF
    for i in range(out.shape[0] // OUT_STEP):
        rows = slice(i * OUT_STEP, (i + 1) * OUT_STEP)
        finish(start, c_ref, gain_ref, state_ref, refs[:groups], refs[groups : 2 * groups], out, rows)


def own_output(place, c, gain, state, parts):
    sums, weights = zip(*parts, strict=True)
    args = (place, c, gain, state, *sums, *weights)
    vmem = pl.BlockSpec(memory_space=pltpu.VMEM)
    return pl.pallas_call(
        own_output_kernel,
        in_specs=[pl.BlockSpec(memory_space=pltpu.SMEM)] + [vmem] * (len(args) - 1),
        out_specs=vmem,
        out_shape=jax.ShapeDtypeStruct((c.shape[0], HALF), BF16),
        name="own_output",
        compiler_params=pltpu.CompilerParams(vmem_limit_bytes=LIMIT),
    )(*args)


def output_kernel(place, c_ref, gain_ref, state_ref, own, *refs):
    groups = HALF // GROUP
    out_hbm, out, own_sem, sems = refs[-4:]
    start = (1 - place[CORE]) * HALF
    own_lanes = pl.ds(pl.multiple_of(place[CORE] * HALF, HALF), HALF)
    lanes = pl.ds(pl.multiple_of(start, HALF), HALF)
    copies = [pltpu.make_async_copy(own, out_hbm.at[:, own_lanes], own_sem)]
    copies[0].start()
    for i in range(out.shape[0] // OUT_STEP):
        rows = slice(i * OUT_STEP, (i + 1) * OUT_STEP)
        finish(start, c_ref, gain_ref, state_ref, refs[:groups], refs[groups : 2 * groups], out, rows)
        where = pl.ds(i * OUT_STEP, OUT_STEP)
        copies.append(pltpu.make_async_copy(out.at[where], out_hbm.at[where, lanes], sems.at[i]))
        copies[-1].start()
    for copy in copies:
        copy.wait()


def output(place, c, gain, state, own, parts):
    tokens = c.shape[0]
    sums, weights = zip(*parts, strict=True)
    args = (place, c, gain, state, own, *sums, *weights)
    vmem = pl.BlockSpec(memory_space=pltpu.VMEM)
    return pl.pallas_call(
        output_kernel,
        in_specs=[pl.BlockSpec(memory_space=pltpu.SMEM)] + [vmem] * (len(args) - 1),
        out_specs=pl.BlockSpec(memory_space=pl.ANY),
        out_shape=jax.ShapeDtypeStruct((tokens, WIDTH), BF16),
        scratch_shapes=[
            pltpu.VMEM((tokens, HALF), BF16),
            pltpu.SemaphoreType.DMA,
            pltpu.SemaphoreType.DMA((tokens // OUT_STEP,)),
        ],
        name="output",
        compiler_params=pltpu.CompilerParams(vmem_limit_bytes=LIMIT),
    )(*args)


def device_of(z, y, x, core):
    return ((z * 4 + y) * 4 + x) * 2 + core


def moved(value, axis, shift):
    sizes = (4, 4, 4, 2)
    pairs = []
    for z in range(4):
        for y in range(4):
            for x in range(4):
                for core in range(2):
                    to = [z, y, x, core]
                    to[axis] = (to[axis] + shift) % sizes[axis]
                    pairs.append((device_of(z, y, x, core), device_of(*to)))
    return lax.ppermute(value, ("grp", "dev"), pairs)


def on_device(x, gate, b, c, decay, d_skip, norm_gain):
    z, r = lax.axis_index("grp"), lax.axis_index("dev")
    place = jnp.stack([z, r // 8, (r // 2) % 4, r % 2]).astype(jnp.int32)
    piece, chunk = (TILES + 1, 8, 128), (QUARTER, HALF)

    x_send, x_keep, factors = decay_factors(place, x, decay)
    send = end_state(False, place, x_send, b, factors)
    recv = moved(send, CORE, 1)
    keep = end_state(True, place, x_keep, b, factors)
    keep, recv = lax.optimization_barrier((keep, recv))
    parts = []
    far_last = (0, 2, 1)

    def work(count, order, *arrived):
        for _ in range(count):
            part = len(parts)
            half = x_keep if part < HALF // GROUP else x_send
            parts.append(local(part, place, d_skip, half, *shared))
        begun = [arrived[i] for i in order]
        begun, parts[-count:] = lax.optimization_barrier((begun, parts[-count:]))
        return [begun[order.index(i)] for i in range(3)]

    u0, *sends = small_call(pair_kernel, "pair", place, (keep, recv), [piece] * 4)
    shared = prepare(gate, b, c, decay)
    lines = [u0] + list(work(1, far_last, *[moved(v, X, s + 1) for s, v in enumerate(sends)]))
    (v0,) = small_call(line_kernel, "line", place, lines, [piece])
    columns = [v0] + list(work(2, far_last, *[moved(v0, Y, s) for s in (1, 2, 3)]))
    w0, before = small_call(plane_kernel, "plane", place, columns, [piece] * 2)
    planes = [w0] + list(work(2, far_last, *[moved(w0, Z, s) for s in (1, 2, 3)]))
    e0, *sends = small_call(enter_kernel, "enter", place, planes + [before] + lines, [chunk] * 4)
    entering = [e0] + list(work(1, (0, 1, 2), *[moved(v, X, s + 1) for s, v in enumerate(sends)]))
    own, send = small_call(chip_kernel, "chip", place, entering + [keep, recv], [(STATE, HALF)] * 2)
    other = moved(send, CORE, 1)
    half = len(parts) // 2
    gain = norm_gain[None]
    own = own_output(place, c, gain, own, parts[:half])
    own, other = lax.optimization_barrier((own, other))
    return output(place, c, gain, other, own, parts[half:])


def solution(mesh):
    return jax.shard_map(
        on_device,
        mesh=mesh,
        in_specs=(
            P(("grp", "dev"), None),
            P(("grp", "dev"), None),
            P(("grp", "dev"), None),
            P(("grp", "dev"), None),
            P(None, ("grp", "dev")),
            P(),
            P(),
        ),
        out_specs=P(("grp", "dev"), None),
        check_vma=False,
    )
```

```python
import functools

import jax
import jax.numpy as jnp
from jax import lax
from jax.experimental import pallas as pl
from jax.experimental.pallas import tpu as pltpu
from jax.sharding import PartitionSpec as P

HEADS = 24
HEAD = 64
STATE = 128
WIDTH = HEADS * HEAD
HALF = WIDTH // 2
SUB = 128
STEP = 256
GROUP = 256
ROWS = STATE + 8
SHIFT = 74
SHIFT_LOG = 51.29289136
OUT_STEP = 256
FETCH = 2048
QUARTER = STATE // 4
TILES = QUARTER // 8 * (HALF // 128)
FETCH_LIMIT = 42 * 1024 * 1024
PREPARE_LIMIT = 40 * 1024 * 1024
LIMIT = 18 * 1024 * 1024
SMALL_LIMIT = 6 * 1024 * 1024
F32 = jnp.float32
BF16 = jnp.bfloat16


def dot(a, b, dims=((1,), (0,))):
    return lax.dot_general(a, b, (dims, ((), ())), preferred_element_type=F32)


def iota(shape, dim):
    return lax.broadcasted_iota(jnp.int32, shape, dim)


def three(v):
    high = v.astype(BF16)
    rest = v - high.astype(F32)
    middle = rest.astype(BF16)
    low = (rest - middle.astype(F32)).astype(BF16)
    return high, middle, low


def spread_parts(v):
    high, middle, low = three(v)
    lane = iota(v.shape, 1)
    picked = jnp.where(
        lane < HEADS, high.astype(F32), jnp.where(lane < 2 * HEADS, middle.astype(F32), low.astype(F32))
    )
    return picked.astype(BF16)


def decay_sums(matrix, decay):
    high, middle, low = three(decay)
    nt = ((1,), (1,))
    return dot(matrix, high, nt) + (dot(matrix, middle, nt) + dot(matrix, low, nt))


def spread_matrix(start, width):
    k, lane = iota((3 * HEADS, width), 0), start + iota((3 * HEADS, width), 1)
    return jnp.where(k % HEADS == lane // HEAD, 1.0, 0.0).astype(BF16)


def half_copies(place, mine, source, target, sems):
    start = pl.multiple_of((place[CORE] if mine else 1 - place[CORE]) * HALF, HALF)
    copies = []
    for i in range(target.shape[0] // FETCH):
        rows = pl.ds(i * FETCH, FETCH)
        copies.append(pltpu.make_async_copy(source.at[rows, pl.ds(start, HALF)], target.at[rows], sems.at[i]))
    return copies


def factors_kernel(place, x_hbm, decay, x_send, x_keep, factors, sems):
    copies = half_copies(place, False, x_hbm, x_send, sems.at[0]) + half_copies(place, True, x_hbm, x_keep, sems.at[1])
    for copy in copies:
        copy.start()
    tokens = decay.shape[1]
    steps = tokens // STEP
    row, col = iota((STEP + 16, STEP), 0), iota((STEP + 16, STEP), 1)
    later = jnp.where((col > row) | (row >= STEP), 1.0, 0.0).astype(BF16)
    sums = []
    for i in range(steps):
        part = decay[:, i * STEP : (i + 1) * STEP]
        sums.append(decay_sums(later, jnp.concatenate([part] * 3, axis=0)))
    after = jnp.zeros((1, 3 * HEADS), F32)
    for i in reversed(range(steps)):
        factors[i * STEP : (i + 1) * STEP] = spread_parts(jnp.exp(sums[i][:STEP] + after))
        after = after + sums[i][STEP : STEP + 1]
    factors[tokens:] = spread_parts(jnp.exp(jnp.broadcast_to(after, (16, 3 * HEADS))))
    for copy in copies:
        copy.wait()


def decay_factors(place, x, decay):
    tokens = x.shape[0]
    vmem = pl.BlockSpec(memory_space=pltpu.VMEM)
    return pl.pallas_call(
        factors_kernel,
        in_specs=[pl.BlockSpec(memory_space=pltpu.SMEM), pl.BlockSpec(memory_space=pl.ANY), vmem],
        out_specs=[vmem] * 3,
        out_shape=[
            jax.ShapeDtypeStruct((tokens, HALF), BF16),
            jax.ShapeDtypeStruct((tokens, HALF), BF16),
            jax.ShapeDtypeStruct((tokens + 16, 3 * HEADS), BF16),
        ],
        scratch_shapes=[pltpu.SemaphoreType.DMA((2, tokens // FETCH))],
        name="decay_factors",
        compiler_params=pltpu.CompilerParams(vmem_limit_bytes=FETCH_LIMIT),
    )(place, x, decay)


def half_state(x, b, factors, scaled, start, out):
    spread = spread_matrix(start, HALF)
    tokens = x.shape[0]
    for i in range(tokens // STEP):
        rows = slice(i * STEP, (i + 1) * STEP)
        scaled[rows] = (x[rows].astype(F32) * dot(factors[rows], spread)).astype(BF16)
    out[:STATE] = dot(b[...], scaled[...], ((0,), (0,)))
    out[STATE:] = dot(factors[tokens:], spread)[:8]


def state_kernel(mine, place, x, b, factors, out, scaled):
    half_state(x, b, factors, scaled, (place[CORE] if mine else 1 - place[CORE]) * HALF, out)


def end_state(mine, place, x, b, factors):
    vmem = pl.BlockSpec(memory_space=pltpu.VMEM)
    return pl.pallas_call(
        functools.partial(state_kernel, mine),
        in_specs=[pl.BlockSpec(memory_space=pltpu.SMEM)] + [vmem] * 3,
        out_specs=vmem,
        out_shape=jax.ShapeDtypeStruct((ROWS, HALF), F32),
        scratch_shapes=[pltpu.VMEM(x.shape, BF16)],
        name="end_state",
        compiler_params=pltpu.CompilerParams(vmem_limit_bytes=LIMIT),
    )(place, x, b, factors)


def small_call(kernel, name, place, args, outs):
    vmem = pl.BlockSpec(memory_space=pltpu.VMEM)
    return pl.pallas_call(
        kernel,
        in_specs=[pl.BlockSpec(memory_space=pltpu.SMEM)] + [vmem] * len(args),
        out_specs=[vmem] * len(outs),
        out_shape=[jax.ShapeDtypeStruct(s, F32) for s in outs],
        name=name,
        compiler_params=pltpu.CompilerParams(vmem_limit_bytes=SMALL_LIMIT),
    )(place, *args)


Z, Y, X, CORE = 0, 1, 2, 3


def parts_of(piece):
    state = piece[:TILES].reshape(QUARTER // 8, HALF // 128, 8, 128)
    decay = [jnp.broadcast_to(piece[TILES, j : j + 1], (8, 128)) for j in range(HALF // 128)]
    return state, jnp.stack(decay)


def set_piece(out, state, decay):
    out[:TILES] = state.reshape(TILES, 8, 128)
    out[TILES] = jnp.zeros((8, 128), F32)
    for j in range(HALF // 128):
        out[TILES, j : j + 1] = decay[j, :1]


def nothing():
    return jnp.zeros((QUARTER // 8, HALF // 128, 8, 128), F32), jnp.ones((HALF // 128, 8, 128), F32)


def pair_kernel(place, keep, recv, own, *sends):
    flip = place[CORE] == 1
    kept, got = keep[STATE : STATE + 8], recv[STATE : STATE + 8]
    late = jnp.where(flip, kept, got)[:1]
    decay = kept * got
    for shift, out in enumerate((own,) + sends):
        chunk = (place[X] + shift) % 4
        rows = pl.ds(pl.multiple_of(chunk * QUARTER, QUARTER), QUARTER)
        a, b = keep[rows], recv[rows]
        total = late * jnp.where(flip, b, a) + jnp.where(flip, a, b)
        out[TILES] = jnp.zeros((8, 128), F32)
        for j in range(HALF // 128):
            lanes = slice(128 * j, 128 * (j + 1))
            out[TILES, j : j + 1] = decay[:1, lanes]
            for i in range(QUARTER // 8):
                out[i * (HALF // 128) + j] = total[8 * i : 8 * (i + 1), lanes]


def ordered(place, axis, refs, j):
    shift = (place[axis] - j + 4) % 4
    value = refs[0][...]
    for s in (1, 2, 3):
        value = jnp.where(shift == s, refs[s][...], value)
    return parts_of(value)


def line_kernel(place, u0, u1, u2, u3, total):
    state, decay = nothing()
    for j in range(4):
        u, u_decay = ordered(place, X, (u0, u1, u2, u3), j)
        state = u_decay * state + u
        decay = decay * u_decay
    set_piece(total, state, decay)


def plane_kernel(place, v0, v1, v2, v3, total, before):
    state, decay = nothing()
    for j in range(4):

        @pl.when(place[Y] == j)
        def _(state=state, decay=decay):
            set_piece(before, state, decay)

        v, v_decay = ordered(place, Y, (v0, v1, v2, v3), j)
        state = v_decay * state + v
        decay = decay * v_decay
    set_piece(total, state, decay)


def enter_kernel(place, w0, w1, w2, w3, before, u0, u1, u2, u3, own, *sends):
    state, _ = nothing()
    for j in range(3):
        w, w_decay = ordered(place, Z, (w0, w1, w2, w3), j)
        state = jnp.where(j < place[Z], w_decay * state + w, state)
    earlier, decay = parts_of(before[...])
    state = decay * state + earlier
    for j in range(4):
        for shift, out in enumerate((own,) + sends):

            @pl.when((place[X] + shift) % 4 == j)
            def _(state=state, out=out):
                for a in range(QUARTER // 8):
                    for b in range(HALF // 128):
                        out[8 * a : 8 * (a + 1), 128 * b : 128 * (b + 1)] = state[a, b]

        if j < 3:
            u, u_decay = ordered(place, X, (u0, u1, u2, u3), j)
            state = u_decay * state + u


def chip_kernel(place, e0, e1, e2, e3, keep, recv, own, send):
    flip = place[CORE] == 1
    first = jnp.where(flip, recv[STATE : STATE + 1], keep[STATE : STATE + 1])
    for shift, e in enumerate((e0, e1, e2, e3)):
        chunk = (place[X] - shift + 4) % 4
        rows = pl.ds(pl.multiple_of(chunk * QUARTER, QUARTER), QUARTER)
        at_first = e[...]
        at_second = first * at_first + jnp.where(flip, recv[rows], keep[rows])
        own[rows] = jnp.where(flip, at_second, at_first)
        send[rows] = jnp.where(flip, at_first, at_second)


BEFORE = SUB + 16


def prepare_kernel(gate_hbm, b_ref, c_ref, decay_ref, gate, left_ref, b_t_ref, before_ref, after_ref, sem):
    fetch = pltpu.make_async_copy(gate_hbm, gate, sem)
    fetch.start()
    tokens = b_ref.shape[0]
    row, col = iota((SUB, SUB), 0), iota((SUB, SUB), 1)
    causal = col <= row
    upto = jnp.where(causal, 1.0, 0.0).astype(BF16)
    start = jnp.zeros((1, 3 * HEADS), F32)
    for s in range(tokens // SUB):
        rows = slice(s * SUB, (s + 1) * SUB)
        decay = decay_ref[:, rows]
        cumul = decay_sums(upto, jnp.concatenate([decay] * 3, axis=0))
        end = cumul[SUB - 1 : SUB]
        shifted = end + SHIFT_LOG
        ends = [jnp.broadcast_to(v, (8, 3 * HEADS)) for v in (shifted, shifted + start)]
        exponents = [shifted - cumul, *ends, cumul - shifted]
        factors = spread_parts(jnp.exp(jnp.concatenate(exponents, axis=0)))
        before_ref[s * BEFORE : (s + 1) * BEFORE] = factors[:BEFORE]
        after_ref[rows] = factors[BEFORE:]
        start = start + end
        b, c = b_ref[rows], c_ref[rows]
        scores = jnp.where(causal, dot(c, b, ((1,), (1,))), 0.0)
        left_ref[rows, :SUB] = scores.astype(BF16)
        left_ref[rows, SUB:] = c
        b_t_ref[rows] = jnp.transpose(b.astype(F32)).astype(BF16)
    fetch.wait()


def prepare(gate, b, c, decay):
    tokens = b.shape[0]
    subs = tokens // SUB
    vmem = pl.BlockSpec(memory_space=pltpu.VMEM)
    return pl.pallas_call(
        prepare_kernel,
        in_specs=[pl.BlockSpec(memory_space=pltpu.HBM)] + [vmem] * 3,
        out_specs=[vmem] * 5,
        out_shape=[
            jax.ShapeDtypeStruct(gate.shape, BF16),
            jax.ShapeDtypeStruct((tokens, SUB + STATE), BF16),
            jax.ShapeDtypeStruct((tokens, SUB), BF16),
            jax.ShapeDtypeStruct((subs * BEFORE, 3 * HEADS), BF16),
            jax.ShapeDtypeStruct((tokens, 3 * HEADS), BF16),
        ],
        scratch_shapes=[pltpu.SemaphoreType.DMA],
        name="prepare",
        compiler_params=pltpu.CompilerParams(vmem_limit_bytes=PREPARE_LIMIT),
    )(gate, b, c, decay)


def local_kernel(
    part, place, skip_ref, x_ref, gate_ref, left_ref, b_t_ref, before_ref, after_ref, sum_ref, weight_ref,
    scaled, carried,
):
    tokens = x_ref.shape[0]
    group = lax.rem(place[CORE] * (HALF // GROUP) + part, WIDTH // GROUP)
    start = pl.multiple_of(group * GROUP, GROUP)
    lanes = pl.ds(start, GROUP)
    at = part % (HALF // GROUP) * GROUP
    x_lanes = slice(at, at + GROUP)
    spread = spread_matrix(start, GROUP)
    lane = iota((1, GROUP), 1)
    skip = jnp.zeros((1, GROUP), F32)
    for h in range(GROUP // HEAD):
        skip = jnp.where(lane // HEAD == h, skip_ref[group * (GROUP // HEAD) + h], skip)
    state = jnp.zeros((STATE, GROUP), F32)
    down = 2.0**-SHIFT
    before = dot(before_ref[...], spread)
    for s in range(tokens // SUB):
        rows = slice(s * SUB, (s + 1) * SUB)
        wide = before[s * BEFORE : (s + 1) * BEFORE]
        scaled[rows] = (x_ref[rows, x_lanes].astype(F32) * wide[:SUB]).astype(BF16)
        decayed = state * wide[SUB : SUB + 1]
        carried[rows] = decayed.astype(BF16)
        state = (decayed + dot(b_t_ref[rows], scaled[rows])) * down
    after = dot(after_ref[...], spread)
    for s in range(tokens // SUB):
        rows = slice(s * SUB, (s + 1) * SUB)
        own = dot(left_ref[rows], jnp.concatenate([scaled[rows], carried[rows]], axis=0))
        h = 0.5 * gate_ref[rows, lanes].astype(F32)
        silu = h + h * jnp.tanh(h)
        factor = after[rows] * silu
        sum_ref[rows] = own * factor + (skip * x_ref[rows, x_lanes].astype(F32)) * silu
        entering = s * BEFORE + SUB + 8
        weight_ref[rows] = (factor * before[entering : entering + 1]).astype(BF16)


def local(part, place, skip, x, gate, left, b_t, before, after):
    tokens = x.shape[0]
    vmem = pl.BlockSpec(memory_space=pltpu.VMEM)
    return pl.pallas_call(
        functools.partial(local_kernel, part),
        in_specs=[pl.BlockSpec(memory_space=pltpu.SMEM)] * 2 + [vmem] * 6,
        out_specs=[vmem] * 2,
        out_shape=[jax.ShapeDtypeStruct((tokens, GROUP), F32), jax.ShapeDtypeStruct((tokens, GROUP), BF16)],
        scratch_shapes=[pltpu.VMEM((tokens, GROUP), BF16)] * 2,
        name="local",
        compiler_params=pltpu.CompilerParams(vmem_limit_bytes=LIMIT),
    )(place, skip, x, gate, left, b_t, before, after)


def finish(start, c_ref, gain_ref, state_ref, sums, weights, out, rows):
    same = iota((GROUP, GROUP), 0) // HEAD == iota((GROUP, GROUP), 1) // HEAD
    mean = jnp.where(same, 1.0 / HEAD, 0.0).astype(BF16)
    for g in range(HALF // GROUP):
        lanes = slice(g * GROUP, (g + 1) * GROUP)
        gain = gain_ref[:, pl.ds(pl.multiple_of(start + g * GROUP, GROUP), GROUP)]
        entering = dot(c_ref[rows], state_ref[:, lanes].astype(BF16))
        gated = sums[g][rows] + weights[g][rows].astype(F32) * entering
        square = dot((gated * gated).astype(BF16), mean)
        out[rows, lanes] = (gated * lax.rsqrt(square + 1e-5) * gain).astype(BF16)


def own_output_kernel(place, c_ref, gain_ref, state_ref, *refs):
    groups = HALF // GROUP
    out = refs[-1]
    start = place[CORE] * HALF
    for i in range(out.shape[0] // OUT_STEP):
        rows = slice(i * OUT_STEP, (i + 1) * OUT_STEP)
        finish(start, c_ref, gain_ref, state_ref, refs[:groups], refs[groups : 2 * groups], out, rows)


def own_output(place, c, gain, state, parts):
    sums, weights = zip(*parts, strict=True)
    args = (place, c, gain, state, *sums, *weights)
    vmem = pl.BlockSpec(memory_space=pltpu.VMEM)
    return pl.pallas_call(
        own_output_kernel,
        in_specs=[pl.BlockSpec(memory_space=pltpu.SMEM)] + [vmem] * (len(args) - 1),
        out_specs=vmem,
        out_shape=jax.ShapeDtypeStruct((c.shape[0], HALF), BF16),
        name="own_output",
        compiler_params=pltpu.CompilerParams(vmem_limit_bytes=LIMIT),
    )(*args)


def output_kernel(place, c_ref, gain_ref, state_ref, own, *refs):
    groups = HALF // GROUP
    out_hbm, out, own_sem, sems = refs[-4:]
    start = (1 - place[CORE]) * HALF
    own_lanes = pl.ds(pl.multiple_of(place[CORE] * HALF, HALF), HALF)
    lanes = pl.ds(pl.multiple_of(start, HALF), HALF)
    copies = [pltpu.make_async_copy(own, out_hbm.at[:, own_lanes], own_sem)]
    copies[0].start()
    for i in range(out.shape[0] // OUT_STEP):
        rows = slice(i * OUT_STEP, (i + 1) * OUT_STEP)
        finish(start, c_ref, gain_ref, state_ref, refs[:groups], refs[groups : 2 * groups], out, rows)
        where = pl.ds(i * OUT_STEP, OUT_STEP)
        copies.append(pltpu.make_async_copy(out.at[where], out_hbm.at[where, lanes], sems.at[i]))
        copies[-1].start()
    for copy in copies:
        copy.wait()


def output(place, c, gain, state, own, parts):
    tokens = c.shape[0]
    sums, weights = zip(*parts, strict=True)
    args = (place, c, gain, state, own, *sums, *weights)
    vmem = pl.BlockSpec(memory_space=pltpu.VMEM)
    return pl.pallas_call(
        output_kernel,
        in_specs=[pl.BlockSpec(memory_space=pltpu.SMEM)] + [vmem] * (len(args) - 1),
        out_specs=pl.BlockSpec(memory_space=pl.ANY),
        out_shape=jax.ShapeDtypeStruct((tokens, WIDTH), BF16),
        scratch_shapes=[
            pltpu.VMEM((tokens, HALF), BF16),
            pltpu.SemaphoreType.DMA,
            pltpu.SemaphoreType.DMA((tokens // OUT_STEP,)),
        ],
        name="output",
        compiler_params=pltpu.CompilerParams(vmem_limit_bytes=LIMIT),
    )(*args)


def device_of(z, y, x, core):
    return ((z * 4 + y) * 4 + x) * 2 + core


def moved(value, axis, shift):
    sizes = (4, 4, 4, 2)
    pairs = []
    for z in range(4):
        for y in range(4):
            for x in range(4):
                for core in range(2):
                    to = [z, y, x, core]
                    to[axis] = (to[axis] + shift) % sizes[axis]
                    pairs.append((device_of(z, y, x, core), device_of(*to)))
    return lax.ppermute(value, ("grp", "dev"), pairs)


def on_device(x, gate, b, c, decay, d_skip, norm_gain):
    z, r = lax.axis_index("grp"), lax.axis_index("dev")
    place = jnp.stack([z, r // 8, (r // 2) % 4, r % 2]).astype(jnp.int32)
    piece, chunk = (TILES + 1, 8, 128), (QUARTER, HALF)

    x_send, x_keep, factors = decay_factors(place, x, decay)
    send = end_state(False, place, x_send, b, factors)
    recv = moved(send, CORE, 1)
    keep = end_state(True, place, x_keep, b, factors)
    keep, recv = lax.optimization_barrier((keep, recv))
    parts = []
    far_last = (0, 2, 1)

    def work(count, order, *arrived):
        for _ in range(count):
            part = len(parts)
            half = x_keep if part < HALF // GROUP else x_send
            parts.append(local(part, place, d_skip, half, *shared))
        begun = [arrived[i] for i in order]
        begun, parts[-count:] = lax.optimization_barrier((begun, parts[-count:]))
        return [begun[order.index(i)] for i in range(3)]

    u0, *sends = small_call(pair_kernel, "pair", place, (keep, recv), [piece] * 4)
    shared = prepare(gate, b, c, decay)
    lines = [u0] + list(work(1, far_last, *[moved(v, X, s + 1) for s, v in enumerate(sends)]))
    (v0,) = small_call(line_kernel, "line", place, lines, [piece])
    columns = [v0] + list(work(2, far_last, *[moved(v0, Y, s) for s in (1, 2, 3)]))
    w0, before = small_call(plane_kernel, "plane", place, columns, [piece] * 2)
    planes = [w0] + list(work(2, far_last, *[moved(w0, Z, s) for s in (1, 2, 3)]))
    e0, *sends = small_call(enter_kernel, "enter", place, planes + [before] + lines, [chunk] * 4)
    entering = [e0] + list(work(1, (1, 0, 2), *[moved(v, X, s + 1) for s, v in enumerate(sends)]))
    own, send = small_call(chip_kernel, "chip", place, entering + [keep, recv], [(STATE, HALF)] * 2)
    other = moved(send, CORE, 1)
    half = len(parts) // 2
    gain = norm_gain[None]
    own = own_output(place, c, gain, own, parts[:half])
    own, other = lax.optimization_barrier((own, other))
    return output(place, c, gain, other, own, parts[half:])


def solution(mesh):
    return jax.shard_map(
        on_device,
        mesh=mesh,
        in_specs=(
            P(("grp", "dev"), None),
            P(("grp", "dev"), None),
            P(("grp", "dev"), None),
            P(("grp", "dev"), None),
            P(None, ("grp", "dev")),
            P(),
            P(),
        ),
        out_specs=P(("grp", "dev"), None),
        check_vma=False,
    )
```

```python
import functools

import jax
import jax.numpy as jnp
from jax import lax
from jax.experimental import pallas as pl
from jax.experimental.pallas import tpu as pltpu
from jax.sharding import PartitionSpec as P

HEADS = 24
HEAD = 64
STATE = 128
WIDTH = HEADS * HEAD
HALF = WIDTH // 2
SUB = 128
STEP = 256
GROUP = 256
ROWS = STATE + 8
SHIFT = 74
SHIFT_LOG = 51.29289136
OUT_STEP = 256
FETCH = 2048
QUARTER = STATE // 4
TILES = QUARTER // 8 * (HALF // 128)
FETCH_LIMIT = 42 * 1024 * 1024
PREPARE_LIMIT = 40 * 1024 * 1024
LIMIT = 18 * 1024 * 1024
SMALL_LIMIT = 6 * 1024 * 1024
F32 = jnp.float32
BF16 = jnp.bfloat16


def dot(a, b, dims=((1,), (0,))):
    return lax.dot_general(a, b, (dims, ((), ())), preferred_element_type=F32)


def iota(shape, dim):
    return lax.broadcasted_iota(jnp.int32, shape, dim)


def three(v):
    high = v.astype(BF16)
    rest = v - high.astype(F32)
    middle = rest.astype(BF16)
    low = (rest - middle.astype(F32)).astype(BF16)
    return high, middle, low


def spread_parts(v):
    high, middle, low = three(v)
    lane = iota(v.shape, 1)
    picked = jnp.where(
        lane < HEADS, high.astype(F32), jnp.where(lane < 2 * HEADS, middle.astype(F32), low.astype(F32))
    )
    return picked.astype(BF16)


def decay_sums(matrix, decay):
    high, middle, low = three(decay)
    nt = ((1,), (1,))
    return dot(matrix, high, nt) + (dot(matrix, middle, nt) + dot(matrix, low, nt))


def spread_matrix(start, width):
    k, lane = iota((3 * HEADS, width), 0), start + iota((3 * HEADS, width), 1)
    return jnp.where(k % HEADS == lane // HEAD, 1.0, 0.0).astype(BF16)


def half_copies(place, mine, source, target, sems):
    start = pl.multiple_of((place[CORE] if mine else 1 - place[CORE]) * HALF, HALF)
    copies = []
    for i in range(target.shape[0] // FETCH):
        rows = pl.ds(i * FETCH, FETCH)
        copies.append(pltpu.make_async_copy(source.at[rows, pl.ds(start, HALF)], target.at[rows], sems.at[i]))
    return copies


def factors_kernel(place, x_hbm, decay, x_send, x_keep, factors, sems):
    copies = half_copies(place, False, x_hbm, x_send, sems.at[0]) + half_copies(place, True, x_hbm, x_keep, sems.at[1])
    for copy in copies:
        copy.start()
    tokens = decay.shape[1]
    steps = tokens // STEP
    row, col = iota((STEP + 16, STEP), 0), iota((STEP + 16, STEP), 1)
    later = jnp.where((col > row) | (row >= STEP), 1.0, 0.0).astype(BF16)
    sums = []
    for i in range(steps):
        part = decay[:, i * STEP : (i + 1) * STEP]
        sums.append(decay_sums(later, jnp.concatenate([part] * 3, axis=0)))
    after = jnp.zeros((1, 3 * HEADS), F32)
    for i in reversed(range(steps)):
        factors[i * STEP : (i + 1) * STEP] = spread_parts(jnp.exp(sums[i][:STEP] + after))
        after = after + sums[i][STEP : STEP + 1]
    factors[tokens:] = spread_parts(jnp.exp(jnp.broadcast_to(after, (16, 3 * HEADS))))
    for copy in copies:
        copy.wait()


def decay_factors(place, x, decay):
    tokens = x.shape[0]
    vmem = pl.BlockSpec(memory_space=pltpu.VMEM)
    return pl.pallas_call(
        factors_kernel,
        in_specs=[pl.BlockSpec(memory_space=pltpu.SMEM), pl.BlockSpec(memory_space=pl.ANY), vmem],
        out_specs=[vmem] * 3,
        out_shape=[
            jax.ShapeDtypeStruct((tokens, HALF), BF16),
            jax.ShapeDtypeStruct((tokens, HALF), BF16),
            jax.ShapeDtypeStruct((tokens + 16, 3 * HEADS), BF16),
        ],
        scratch_shapes=[pltpu.SemaphoreType.DMA((2, tokens // FETCH))],
        name="decay_factors",
        compiler_params=pltpu.CompilerParams(vmem_limit_bytes=FETCH_LIMIT),
    )(place, x, decay)


def half_state(x, b, factors, scaled, start, out):
    spread = spread_matrix(start, HALF)
    tokens = x.shape[0]
    for i in range(tokens // STEP):
        rows = slice(i * STEP, (i + 1) * STEP)
        scaled[rows] = (x[rows].astype(F32) * dot(factors[rows], spread)).astype(BF16)
    out[:STATE] = dot(b[...], scaled[...], ((0,), (0,)))
    out[STATE:] = dot(factors[tokens:], spread)[:8]


def state_kernel(mine, place, x, b, factors, out, scaled):
    half_state(x, b, factors, scaled, (place[CORE] if mine else 1 - place[CORE]) * HALF, out)


def end_state(mine, place, x, b, factors):
    vmem = pl.BlockSpec(memory_space=pltpu.VMEM)
    return pl.pallas_call(
        functools.partial(state_kernel, mine),
        in_specs=[pl.BlockSpec(memory_space=pltpu.SMEM)] + [vmem] * 3,
        out_specs=vmem,
        out_shape=jax.ShapeDtypeStruct((ROWS, HALF), F32),
        scratch_shapes=[pltpu.VMEM(x.shape, BF16)],
        name="end_state",
        compiler_params=pltpu.CompilerParams(vmem_limit_bytes=LIMIT),
    )(place, x, b, factors)


def small_call(kernel, name, place, args, outs):
    vmem = pl.BlockSpec(memory_space=pltpu.VMEM)
    return pl.pallas_call(
        kernel,
        in_specs=[pl.BlockSpec(memory_space=pltpu.SMEM)] + [vmem] * len(args),
        out_specs=[vmem] * len(outs),
        out_shape=[jax.ShapeDtypeStruct(s, F32) for s in outs],
        name=name,
        compiler_params=pltpu.CompilerParams(vmem_limit_bytes=SMALL_LIMIT),
    )(place, *args)


Z, Y, X, CORE = 0, 1, 2, 3


def parts_of(piece):
    state = piece[:TILES].reshape(QUARTER // 8, HALF // 128, 8, 128)
    decay = [jnp.broadcast_to(piece[TILES, j : j + 1], (8, 128)) for j in range(HALF // 128)]
    return state, jnp.stack(decay)


def set_piece(out, state, decay):
    out[:TILES] = state.reshape(TILES, 8, 128)
    out[TILES] = jnp.zeros((8, 128), F32)
    for j in range(HALF // 128):
        out[TILES, j : j + 1] = decay[j, :1]


def nothing():
    return jnp.zeros((QUARTER // 8, HALF // 128, 8, 128), F32), jnp.ones((HALF // 128, 8, 128), F32)


def pair_kernel(place, keep, recv, own, *sends):
    flip = place[CORE] == 1
    kept, got = keep[STATE : STATE + 8], recv[STATE : STATE + 8]
    late = jnp.where(flip, kept, got)[:1]
    decay = kept * got
    for shift, out in enumerate((own,) + sends):
        chunk = (place[X] + shift) % 4
        rows = pl.ds(pl.multiple_of(chunk * QUARTER, QUARTER), QUARTER)
        a, b = keep[rows], recv[rows]
        total = late * jnp.where(flip, b, a) + jnp.where(flip, a, b)
        out[TILES] = jnp.zeros((8, 128), F32)
        for j in range(HALF // 128):
            lanes = slice(128 * j, 128 * (j + 1))
            out[TILES, j : j + 1] = decay[:1, lanes]
            for i in range(QUARTER // 8):
                out[i * (HALF // 128) + j] = total[8 * i : 8 * (i + 1), lanes]


def ordered(place, axis, refs, j):
    shift = (place[axis] - j + 4) % 4
    value = refs[0][...]
    for s in (1, 2, 3):
        value = jnp.where(shift == s, refs[s][...], value)
    return parts_of(value)


def line_kernel(place, u0, u1, u2, u3, total):
    state, decay = nothing()
    for j in range(4):
        u, u_decay = ordered(place, X, (u0, u1, u2, u3), j)
        state = u_decay * state + u
        decay = decay * u_decay
    set_piece(total, state, decay)


def plane_kernel(place, v0, v1, v2, v3, total, before):
    state, decay = nothing()
    for j in range(4):

        @pl.when(place[Y] == j)
        def _(state=state, decay=decay):
            set_piece(before, state, decay)

        v, v_decay = ordered(place, Y, (v0, v1, v2, v3), j)
        state = v_decay * state + v
        decay = decay * v_decay
    set_piece(total, state, decay)


def enter_kernel(place, w0, w1, w2, w3, before, u0, u1, u2, u3, own, *sends):
    state, _ = nothing()
    for j in range(3):
        w, w_decay = ordered(place, Z, (w0, w1, w2, w3), j)
        state = jnp.where(j < place[Z], w_decay * state + w, state)
    earlier, decay = parts_of(before[...])
    state = decay * state + earlier
    for j in range(4):
        for shift, out in enumerate((own,) + sends):

            @pl.when((place[X] + shift) % 4 == j)
            def _(state=state, out=out):
                for a in range(QUARTER // 8):
                    for b in range(HALF // 128):
                        out[8 * a : 8 * (a + 1), 128 * b : 128 * (b + 1)] = state[a, b]

        if j < 3:
            u, u_decay = ordered(place, X, (u0, u1, u2, u3), j)
            state = u_decay * state + u


def chip_kernel(place, e0, e1, e2, e3, keep, recv, own, send):
    flip = place[CORE] == 1
    first = jnp.where(flip, recv[STATE : STATE + 1], keep[STATE : STATE + 1])
    for shift, e in enumerate((e0, e1, e2, e3)):
        chunk = (place[X] - shift + 4) % 4
        rows = pl.ds(pl.multiple_of(chunk * QUARTER, QUARTER), QUARTER)
        at_first = e[...]
        at_second = first * at_first + jnp.where(flip, recv[rows], keep[rows])
        own[rows] = jnp.where(flip, at_second, at_first)
        send[rows] = jnp.where(flip, at_first, at_second)


BEFORE = SUB + 16


def prepare_kernel(gate_hbm, b_ref, c_ref, decay_ref, gate, left_ref, b_t_ref, before_ref, after_ref, sem):
    fetch = pltpu.make_async_copy(gate_hbm, gate, sem)
    fetch.start()
    tokens = b_ref.shape[0]
    row, col = iota((SUB, SUB), 0), iota((SUB, SUB), 1)
    causal = col <= row
    upto = jnp.where(causal, 1.0, 0.0).astype(BF16)
    start = jnp.zeros((1, 3 * HEADS), F32)
    for s in range(tokens // SUB):
        rows = slice(s * SUB, (s + 1) * SUB)
        decay = decay_ref[:, rows]
        cumul = decay_sums(upto, jnp.concatenate([decay] * 3, axis=0))
        end = cumul[SUB - 1 : SUB]
        shifted = end + SHIFT_LOG
        ends = [jnp.broadcast_to(v, (8, 3 * HEADS)) for v in (shifted, shifted + start)]
        exponents = [shifted - cumul, *ends, cumul - shifted]
        factors = spread_parts(jnp.exp(jnp.concatenate(exponents, axis=0)))
        before_ref[s * BEFORE : (s + 1) * BEFORE] = factors[:BEFORE]
        after_ref[rows] = factors[BEFORE:]
        start = start + end
        b, c = b_ref[rows], c_ref[rows]
        scores = jnp.where(causal, dot(c, b, ((1,), (1,))), 0.0)
        left_ref[rows, :SUB] = scores.astype(BF16)
        left_ref[rows, SUB:] = c
        b_t_ref[rows] = jnp.transpose(b.astype(F32)).astype(BF16)
    fetch.wait()


def prepare(gate, b, c, decay):
    tokens = b.shape[0]
    subs = tokens // SUB
    vmem = pl.BlockSpec(memory_space=pltpu.VMEM)
    return pl.pallas_call(
        prepare_kernel,
        in_specs=[pl.BlockSpec(memory_space=pltpu.HBM)] + [vmem] * 3,
        out_specs=[vmem] * 5,
        out_shape=[
            jax.ShapeDtypeStruct(gate.shape, BF16),
            jax.ShapeDtypeStruct((tokens, SUB + STATE), BF16),
            jax.ShapeDtypeStruct((tokens, SUB), BF16),
            jax.ShapeDtypeStruct((subs * BEFORE, 3 * HEADS), BF16),
            jax.ShapeDtypeStruct((tokens, 3 * HEADS), BF16),
        ],
        scratch_shapes=[pltpu.SemaphoreType.DMA],
        name="prepare",
        compiler_params=pltpu.CompilerParams(vmem_limit_bytes=PREPARE_LIMIT),
    )(gate, b, c, decay)


def local_kernel(
    part, place, skip_ref, x_ref, gate_ref, left_ref, b_t_ref, before_ref, after_ref, sum_ref, weight_ref,
    scaled, carried,
):
    tokens = x_ref.shape[0]
    group = lax.rem(place[CORE] * (HALF // GROUP) + part, WIDTH // GROUP)
    start = pl.multiple_of(group * GROUP, GROUP)
    lanes = pl.ds(start, GROUP)
    at = part % (HALF // GROUP) * GROUP
    x_lanes = slice(at, at + GROUP)
    spread = spread_matrix(start, GROUP)
    lane = iota((1, GROUP), 1)
    skip = jnp.zeros((1, GROUP), F32)
    for h in range(GROUP // HEAD):
        skip = jnp.where(lane // HEAD == h, skip_ref[group * (GROUP // HEAD) + h], skip)
    state = jnp.zeros((STATE, GROUP), F32)
    down = 2.0**-SHIFT
    before = dot(before_ref[...], spread)
    for s in range(tokens // SUB):
        rows = slice(s * SUB, (s + 1) * SUB)
        wide = before[s * BEFORE : (s + 1) * BEFORE]
        scaled[rows] = (x_ref[rows, x_lanes].astype(F32) * wide[:SUB]).astype(BF16)
        decayed = state * wide[SUB : SUB + 1]
        carried[rows] = decayed.astype(BF16)
        state = (decayed + dot(b_t_ref[rows], scaled[rows])) * down
    after = dot(after_ref[...], spread)
    for s in range(tokens // SUB):
        rows = slice(s * SUB, (s + 1) * SUB)
        own = dot(left_ref[rows], jnp.concatenate([scaled[rows], carried[rows]], axis=0))
        h = 0.5 * gate_ref[rows, lanes].astype(F32)
        silu = h + h * jnp.tanh(h)
        factor = after[rows] * silu
        sum_ref[rows] = own * factor + (skip * x_ref[rows, x_lanes].astype(F32)) * silu
        entering = s * BEFORE + SUB + 8
        weight_ref[rows] = (factor * before[entering : entering + 1]).astype(BF16)


def local(part, place, skip, x, gate, left, b_t, before, after):
    tokens = x.shape[0]
    vmem = pl.BlockSpec(memory_space=pltpu.VMEM)
    return pl.pallas_call(
        functools.partial(local_kernel, part),
        in_specs=[pl.BlockSpec(memory_space=pltpu.SMEM)] * 2 + [vmem] * 6,
        out_specs=[vmem] * 2,
        out_shape=[jax.ShapeDtypeStruct((tokens, GROUP), F32), jax.ShapeDtypeStruct((tokens, GROUP), BF16)],
        scratch_shapes=[pltpu.VMEM((tokens, GROUP), BF16)] * 2,
        name="local",
        compiler_params=pltpu.CompilerParams(vmem_limit_bytes=LIMIT),
    )(place, skip, x, gate, left, b_t, before, after)


def finish(start, c_ref, gain_ref, state_ref, sums, weights, out, rows):
    same = iota((GROUP, GROUP), 0) // HEAD == iota((GROUP, GROUP), 1) // HEAD
    mean = jnp.where(same, 1.0 / HEAD, 0.0).astype(BF16)
    for g in range(HALF // GROUP):
        lanes = slice(g * GROUP, (g + 1) * GROUP)
        gain = gain_ref[:, pl.ds(pl.multiple_of(start + g * GROUP, GROUP), GROUP)]
        entering = dot(c_ref[rows], state_ref[:, lanes].astype(BF16))
        gated = sums[g][rows] + weights[g][rows].astype(F32) * entering
        square = dot((gated * gated).astype(BF16), mean)
        out[rows, lanes] = (gated * lax.rsqrt(square + 1e-5) * gain).astype(BF16)


def own_output_kernel(place, c_ref, gain_ref, state_ref, *refs):
    groups = HALF // GROUP
    out_hbm, out, sems = refs[-3:]
    start = place[CORE] * HALF
    lanes = pl.ds(pl.multiple_of(start, HALF), HALF)
    steps = out.shape[0] // OUT_STEP
    copies = []
    for i in range(steps):
        rows = slice(i * OUT_STEP, (i + 1) * OUT_STEP)
        finish(start, c_ref, gain_ref, state_ref, refs[:groups], refs[groups : 2 * groups], out, rows)
        if i < steps // 2:
            where = pl.ds(i * OUT_STEP, OUT_STEP)
            copies.append(pltpu.make_async_copy(out.at[where], out_hbm.at[where, lanes], sems.at[i]))
            copies[-1].start()
    for copy in copies:
        copy.wait()


def own_output(place, c, gain, state, parts):
    tokens = c.shape[0]
    sums, weights = zip(*parts, strict=True)
    args = (place, c, gain, state, *sums, *weights)
    vmem = pl.BlockSpec(memory_space=pltpu.VMEM)
    return pl.pallas_call(
        own_output_kernel,
        in_specs=[pl.BlockSpec(memory_space=pltpu.SMEM)] + [vmem] * (len(args) - 1),
        out_specs=[pl.BlockSpec(memory_space=pl.ANY), vmem],
        out_shape=[jax.ShapeDtypeStruct((tokens, WIDTH), BF16), jax.ShapeDtypeStruct((tokens, HALF), BF16)],
        scratch_shapes=[pltpu.SemaphoreType.DMA((tokens // OUT_STEP // 2,))],
        name="own_output",
        compiler_params=pltpu.CompilerParams(vmem_limit_bytes=LIMIT),
    )(*args)


def output_kernel(place, c_ref, gain_ref, state_ref, own, *refs):
    groups = HALF // GROUP
    out_hbm, out, own_sem, sems = refs[-4:]
    start = (1 - place[CORE]) * HALF
    own_lanes = pl.ds(pl.multiple_of(place[CORE] * HALF, HALF), HALF)
    lanes = pl.ds(pl.multiple_of(start, HALF), HALF)
    rest = pl.ds(own.shape[0] // 2, own.shape[0] // 2)
    copies = [pltpu.make_async_copy(own.at[rest], out_hbm.at[rest, own_lanes], own_sem)]
    copies[0].start()
    for i in range(out.shape[0] // OUT_STEP):
        rows = slice(i * OUT_STEP, (i + 1) * OUT_STEP)
        finish(start, c_ref, gain_ref, state_ref, refs[:groups], refs[groups : 2 * groups], out, rows)
        where = pl.ds(i * OUT_STEP, OUT_STEP)
        copies.append(pltpu.make_async_copy(out.at[where], out_hbm.at[where, lanes], sems.at[i]))
        copies[-1].start()
    for copy in copies:
        copy.wait()


def output(place, c, gain, state, own, parts, begun):
    tokens = c.shape[0]
    sums, weights = zip(*parts, strict=True)
    args = (place, c, gain, state, own, *sums, *weights)
    vmem = pl.BlockSpec(memory_space=pltpu.VMEM)
    return pl.pallas_call(
        output_kernel,
        in_specs=[pl.BlockSpec(memory_space=pltpu.SMEM)] + [vmem] * (len(args) - 1) + [pl.BlockSpec(memory_space=pl.ANY)],
        out_specs=pl.BlockSpec(memory_space=pl.ANY),
        input_output_aliases={len(args): 0},
        out_shape=jax.ShapeDtypeStruct((tokens, WIDTH), BF16),
        scratch_shapes=[
            pltpu.VMEM((tokens, HALF), BF16),
            pltpu.SemaphoreType.DMA,
            pltpu.SemaphoreType.DMA((tokens // OUT_STEP,)),
        ],
        name="output",
        compiler_params=pltpu.CompilerParams(vmem_limit_bytes=LIMIT),
    )(*args, begun)


def device_of(z, y, x, core):
    return ((z * 4 + y) * 4 + x) * 2 + core


def moved(value, axis, shift):
    sizes = (4, 4, 4, 2)
    pairs = []
    for z in range(4):
        for y in range(4):
            for x in range(4):
                for core in range(2):
                    to = [z, y, x, core]
                    to[axis] = (to[axis] + shift) % sizes[axis]
                    pairs.append((device_of(z, y, x, core), device_of(*to)))
    return lax.ppermute(value, ("grp", "dev"), pairs)


def on_device(x, gate, b, c, decay, d_skip, norm_gain):
    z, r = lax.axis_index("grp"), lax.axis_index("dev")
    place = jnp.stack([z, r // 8, (r // 2) % 4, r % 2]).astype(jnp.int32)
    piece, chunk = (TILES + 1, 8, 128), (QUARTER, HALF)

    x_send, x_keep, factors = decay_factors(place, x, decay)
    send = end_state(False, place, x_send, b, factors)
    recv = moved(send, CORE, 1)
    keep = end_state(True, place, x_keep, b, factors)
    keep, recv = lax.optimization_barrier((keep, recv))
    parts = []
    far_last = (0, 2, 1)

    def work(count, order, *arrived):
        for _ in range(count):
            part = len(parts)
            half = x_keep if part < HALF // GROUP else x_send
            parts.append(local(part, place, d_skip, half, *shared))
        begun = [arrived[i] for i in order]
        begun, parts[-count:] = lax.optimization_barrier((begun, parts[-count:]))
        return [begun[order.index(i)] for i in range(3)]

    u0, *sends = small_call(pair_kernel, "pair", place, (keep, recv), [piece] * 4)
    shared = prepare(gate, b, c, decay)
    lines = [u0] + list(work(1, far_last, *[moved(v, X, s + 1) for s, v in enumerate(sends)]))
    (v0,) = small_call(line_kernel, "line", place, lines, [piece])
    columns = [v0] + list(work(2, far_last, *[moved(v0, Y, s) for s in (1, 2, 3)]))
    w0, before = small_call(plane_kernel, "plane", place, columns, [piece] * 2)
    planes = [w0] + list(work(2, far_last, *[moved(w0, Z, s) for s in (1, 2, 3)]))
    e0, *sends = small_call(enter_kernel, "enter", place, planes + [before] + lines, [chunk] * 4)
    entering = [e0] + list(work(1, (1, 0, 2), *[moved(v, X, s + 1) for s, v in enumerate(sends)]))
    own, send = small_call(chip_kernel, "chip", place, entering + [keep, recv], [(STATE, HALF)] * 2)
    other = moved(send, CORE, 1)
    half = len(parts) // 2
    gain = norm_gain[None]
    begun, own = own_output(place, c, gain, own, parts[:half])
    own, other = lax.optimization_barrier((own, other))
    return output(place, c, gain, other, own, parts[half:], begun)


def solution(mesh):
    return jax.shard_map(
        on_device,
        mesh=mesh,
        in_specs=(
            P(("grp", "dev"), None),
            P(("grp", "dev"), None),
            P(("grp", "dev"), None),
            P(("grp", "dev"), None),
            P(None, ("grp", "dev")),
            P(),
            P(),
        ),
        out_specs=P(("grp", "dev"), None),
        check_vma=False,
    )
```
